128 devices in a mesh: section: 2 (over core), expert: 16 (over y, x), dp: 4 (over z).
Axes of the slice: x: 4, y: 4, z: 4, core: 2. Of those that a mesh axis runs over, the one named last changes fastest.
Arguments:
- tokens: bfloat16 [4, 2048, 2048], P(None, ('expert', 'dp')), may hold values from -6 to 6
- routes: int32 [2, 4, 2048, 2], P('section', None, ('expert', 'dp')), may hold values from 0 to 15, all different within a row; in each aligned block of 32 rows (0 to 31, 32 to 63, ..., all dimensions but the last counted through in order) at most 5 rows name the same one
- gate_probs: float32 [2, 4, 2048, 2], P('section', None, ('expert', 'dp')), may hold values from 0.1 to 1
- w_gate: bfloat16 [2, 16, 2048, 640], P('section', 'expert'), may hold values from -0.125 to 0.125
- w_up: bfloat16 [2, 16, 2048, 640], P('section', 'expert'), may hold values from -0.125 to 0.125
- w_down: bfloat16 [2, 16, 640, 2048], P('section', 'expert'), may hold values from -0.25 to 0.25
- cotangent: bfloat16 [4, 2048, 2048], P(None, ('expert', 'dp')), may hold values from -0.29882812 to 0.29882812
Outputs:
- grad_gate: float32 [2, 16, 2048, 640], P('section', 'expert', 'dp')
- grad_up: float32 [2, 16, 2048, 640], P('section', 'expert', 'dp')
- grad_down: float32 [2, 16, 640, 2048], P('section', 'expert', None, 'dp')
The draws below stay inside these ranges and needn't reach their ends.
Inputs may be any that keep to these rules, and one draw needn't show every extreme that they name: `routes`: in each micro-batch and layer, the 32 token rows of one device (aligned blocks) name each expert at most 5 times, a bound that some block reaches; the 2 experts of a token differ.
All inputs are finite; a program needn't handle non-finite values.
Results may differ from the reference program's by a relative error of at most 0.015.
Values may be sent and summed in bfloat16 or wider, within the bound.
A program may use at most 64 MiB of HBM per device.

```python
import math
import jax
import jax.numpy as jnp
import numpy as np
from jax import lax

D = 2048
FF_DEV = 640
TOP = 2
M = 4
ROWS = 32
EXPERTS = 16
CAP = 5
TOKENS = 2048
N_SECTION = 2
N_EXPERT = 16
N_DP = 4


def steps_of(stream_key, dims, pieces, least, high):
    loudness = 1.0
    for dim, blocks in pieces:
        heights = jax.random.uniform(jax.random.fold_in(jax.random.fold_in(stream_key, 6), dim), (blocks,), jnp.float32, least / len(pieces), high / len(pieces))
        loudness = loudness * jnp.repeat(jnp.exp(heights), dims[dim] // blocks).reshape((-1,) + (1,) * (len(dims) - 1 - dim))
    return loudness


def deal_out(own_key, own, number, rows, number_of, top, reach, slope):
    sequence = jax.random.permutation(own_key, number_of)
    packed, usual = portions_of(number_of, rows * top, reach, slope, True), portions_of(number_of, rows * top, reach, slope, False)
    places = jnp.arange(number_of)

    def named(lengths, rotation):
        used = int((lengths > 0).sum())
        fixed = max(1, used // 4)
        moved = fixed + (places - fixed + rotation * (used - fixed)) % max(1, number_of - fixed)
        return jnp.zeros((number_of,), jnp.int32).at[sequence[jnp.where(places < fixed, places, moved)]].set(jnp.asarray(lengths, jnp.int32))

    lengths = jnp.where(number % 4 == 0, named(packed, number // 4), named(usual, number - number // 4 - 1))
    mixed = jax.random.permutation(jax.random.fold_in(own, 3), number_of)
    source_of, sink = mixed[0:number_of // 2 * 2:2], mixed[1:number_of // 2 * 2:2]
    slack = jnp.minimum(lengths[source_of] - 1, reach - lengths[sink]) // 2
    slack = jnp.where((source_of == sequence[0]) | (sink == sequence[0]) | (lengths[sink] == 0), 0, jnp.maximum(slack, 0))
    moved = jax.random.randint(jax.random.fold_in(own, 4), (number_of // 2,), 0, 1 << 20) % (slack + 1)
    lengths = lengths.at[source_of].add(-moved).at[sink].add(moved)
    members = jnp.searchsorted(jnp.cumsum(lengths), jnp.arange(rows * top), side="right").astype(jnp.int32)
    table = members.reshape(top, rows).T
    table = table[jax.random.permutation(jax.random.fold_in(own, 1), rows)]
    rotation = jax.random.randint(jax.random.fold_in(own, 2), (rows, 1), 0, top)
    return jnp.take_along_axis(table, (jnp.arange(top)[None, :] + rotation) % top, axis=1)


def portions_of(number_of, total, most, slope, full):
    loads = [(1 << 20) // math.isqrt(rank ** slope) + 1 for rank in range(1, number_of + 1)]
    largest = most if full else min(most, max(-(-total // number_of), total * loads[0] // sum(loads)))
    least = 1 if total - largest >= number_of - 1 else 0
    holding, spare = [largest] + [least] * (number_of - 1), total - largest - least * (number_of - 1)
    while spare > 0:
        movable = [i for i in range(1, number_of) if holding[i] < largest] or [i for i in range(1, number_of) if holding[i] < most]
        mass, left = sum([loads[i] for i in movable]), spare
        for i in movable:
            addition = min(most - holding[i], max(1, left * loads[i] // mass), spare)
            holding[i] = holding[i] + addition
            spare = spare - addition
    return np.array(holding)


def centred(stream_key, dims, deviation, reach, cuts=(), held_as=jnp.bfloat16):
    gain = steps_of(stream_key, dims, cuts, -0.22, 0.18) if cuts else 1.0
    result = jax.random.normal(stream_key, dims, jnp.float32) * deviation * gain
    return jnp.minimum(jnp.maximum(result, -reach), reach).astype(held_as)


def setup_inputs(seed: int = 0) -> dict:
    arg_keys = jax.random.split(jax.random.key(seed), 8)
    tokens = centred(arg_keys[0], (M, TOKENS, D), 1.0, 6.0, ((1, 64),))
    routes_keys = jax.random.split(jax.random.fold_in(arg_keys[1], 1), N_SECTION * M * TOKENS // ROWS)
    routes_turns = jax.random.permutation(jax.random.fold_in(arg_keys[1], 3), N_SECTION * M * TOKENS // ROWS)
    routes = jax.vmap(lambda own, number: deal_out(jax.random.fold_in(arg_keys[1], 2), own, number, ROWS, EXPERTS, TOP, CAP, 2))(routes_keys, routes_turns).reshape((N_SECTION, M, TOKENS, TOP))
    gate_probs = jnp.clip(jnp.exp(math.log(1.0) - 2.3025851 * jax.random.uniform(arg_keys[2], (N_SECTION, M, TOKENS, TOP), jnp.float32) ** steps_of(arg_keys[2], (N_SECTION, M, TOKENS, TOP), ((0, 2), (2, 64)), -0.2, 0.2)), 0.1, 1.0)
    w_gate = centred(arg_keys[3], (N_SECTION, EXPERTS, D, FF_DEV), D ** -0.5, 0.125, ((0, 2), (1, 16)))
    w_up = centred(arg_keys[4], (N_SECTION, EXPERTS, D, FF_DEV), D ** -0.5, 0.125, ((0, 2), (1, 16)))
    w_down = centred(arg_keys[5], (N_SECTION, EXPERTS, FF_DEV, D), FF_DEV ** -0.5, 0.25, ((0, 2), (1, 16)))
    cotangent = centred(arg_keys[6], (M, TOKENS, D), 0.05, 0.29882812, ((1, 64),))
    return {"tokens": tokens, "routes": routes, "gate_probs": gate_probs, "w_gate": w_gate, "w_up": w_up, "w_down": w_down, "cotangent": cotangent}


epsilon = 1e-05

def inverse_rms(values):
    return lax.rsqrt(lax.optimization_barrier(jnp.mean(values * values, -1, keepdims=True)) + epsilon)

def route_slots(route_ids):
    flat_ids = route_ids.reshape(-1).astype(jnp.int32)
    one_hot = (flat_ids[:, None] == jnp.arange(EXPERTS, dtype=jnp.int32)[None, :]).astype(jnp.int32)
    earlier = jnp.cumsum(one_hot, 0) - one_hot
    slot_num = lax.optimization_barrier(jnp.sum(earlier * one_hot, 1)).astype(jnp.int32)
    return (flat_ids, slot_num)

def expert_inputs(normed, flat_ids, slot_num):
    buffer_rows = N_EXPERT * N_DP * CAP
    token_of_pair = (jnp.arange(TOKENS * TOP, dtype=jnp.int32) // TOP).astype(jnp.int32)
    table = jnp.full((EXPERTS, buffer_rows), TOKENS, dtype=jnp.int32).at[flat_ids, slot_num].set(token_of_pair)
    padded = jnp.concatenate([normed, jnp.zeros((1, D), normed.dtype)], 0)
    return padded[table]

def pre_activations(rows_in, gate_mats, up_mats):
    rows_f = rows_in.astype(jnp.float32)
    pre_gate = jnp.einsum('ebd,edf->ebf', rows_f, gate_mats.astype(jnp.float32))
    pre_up = jnp.einsum('ebd,edf->ebf', rows_f, up_mats.astype(jnp.float32))
    return (pre_gate, pre_up)

def layer_forward(current, route_ids, probs, gate_mats, up_mats, down_mats):
    current_f = current.astype(jnp.float32)
    normed = (current_f * inverse_rms(current_f)).astype(jnp.bfloat16)
    flat_ids, slot_num = route_slots(route_ids)
    rows_in = expert_inputs(normed, flat_ids, slot_num)
    pre_gate, pre_up = pre_activations(rows_in, gate_mats, up_mats)
    activation = (jax.nn.silu(pre_gate) * pre_up).astype(jnp.bfloat16)
    produced = jnp.einsum('ebf,efd->ebd', activation.astype(jnp.float32), down_mats.astype(jnp.float32)).astype(jnp.bfloat16)
    chosen = produced[flat_ids, slot_num].reshape(TOKENS, TOP, D).astype(jnp.float32)
    return (current_f + lax.optimization_barrier(jnp.sum(probs[:, :, None] * chosen, 1))).astype(jnp.bfloat16)

def layer_backward(current, upstream, route_ids, probs, gate_mats, up_mats, down_mats):
    buffer_rows = N_EXPERT * N_DP * CAP
    current_f = current.astype(jnp.float32)
    scale_rms = inverse_rms(current_f)
    normed = (current_f * scale_rms).astype(jnp.bfloat16)
    flat_ids, slot_num = route_slots(route_ids)
    rows_in = expert_inputs(normed, flat_ids, slot_num)
    pre_gate, pre_up = pre_activations(rows_in, gate_mats, up_mats)
    upstream_f = upstream.astype(jnp.float32)
    scaled = (probs[:, :, None] * upstream_f[:, None, :]).astype(jnp.bfloat16).reshape(TOKENS * TOP, D)
    arrived = jnp.zeros((EXPERTS, buffer_rows, D), jnp.bfloat16).at[flat_ids, slot_num].set(scaled)
    back_hidden = jnp.einsum('ebd,efd->ebf', arrived.astype(jnp.float32), down_mats.astype(jnp.float32))
    sigmoid_gate = jax.nn.sigmoid(pre_gate)
    silu_gate = pre_gate * sigmoid_gate
    d_gate = (back_hidden * pre_up * sigmoid_gate * (1.0 + pre_gate * (1.0 - sigmoid_gate))).astype(jnp.bfloat16)
    d_up = (back_hidden * silu_gate).astype(jnp.bfloat16)
    activation = (silu_gate * pre_up).astype(jnp.bfloat16)
    d_rows = (jnp.einsum('ebf,edf->ebd', d_gate.astype(jnp.float32), gate_mats.astype(jnp.float32)) + jnp.einsum('ebf,edf->ebd', d_up.astype(jnp.float32), up_mats.astype(jnp.float32))).astype(jnp.bfloat16)
    rows_f = rows_in.astype(jnp.float32)
    part_gate = jnp.einsum('ebd,ebf->edf', rows_f, d_gate.astype(jnp.float32))
    part_up = jnp.einsum('ebd,ebf->edf', rows_f, d_up.astype(jnp.float32))
    part_down = jnp.einsum('ebf,ebd->efd', activation.astype(jnp.float32), arrived.astype(jnp.float32))
    d_normed = lax.optimization_barrier(jnp.sum(d_rows[flat_ids, slot_num].reshape(TOKENS, TOP, D).astype(jnp.float32), 1))
    d_current = scale_rms * d_normed - current_f * scale_rms ** 3 * lax.optimization_barrier(jnp.mean(d_normed * current_f, -1, keepdims=True))
    passed = (upstream_f + d_current).astype(jnp.bfloat16)
    return (passed, part_gate, part_up, part_down)

def reference(tokens, routes, gate_probs, w_gate, w_up, w_down, cotangent):
    saved = []
    layer_acts = [tokens[micro_num] for micro_num in range(M)]
    for section_num in range(N_SECTION):
        saved.append(layer_acts)
        layer_acts = [layer_forward(layer_acts[micro_num], routes[section_num, micro_num], gate_probs[section_num, micro_num], w_gate[section_num], w_up[section_num], w_down[section_num]) for micro_num in range(M)]
    upstream = [cotangent[micro_num] for micro_num in range(M)]
    grads_gate = [None] * N_SECTION
    grads_up = [None] * N_SECTION
    grads_down = [None] * N_SECTION
    for section_num in reversed(range(N_SECTION)):
        total_gate = jnp.zeros((EXPERTS, D, FF_DEV), jnp.float32)
        total_up = jnp.zeros((EXPERTS, D, FF_DEV), jnp.float32)
        total_down = jnp.zeros((EXPERTS, FF_DEV, D), jnp.float32)
        next_upstream = []
        for micro_num in range(M):
            passed, part_gate, part_up, part_down = layer_backward(saved[section_num][micro_num], upstream[micro_num], routes[section_num, micro_num], gate_probs[section_num, micro_num], w_gate[section_num], w_up[section_num], w_down[section_num])
            total_gate = total_gate + part_gate
            total_up = total_up + part_up
            total_down = total_down + part_down
            next_upstream.append(passed)
        upstream = next_upstream
        grads_gate[section_num] = total_gate
        grads_up[section_num] = total_up
        grads_down[section_num] = total_down
    return (jnp.stack(grads_gate), jnp.stack(grads_up), jnp.stack(grads_down))
```

```python
import functools
import jax
import jax.numpy as jnp
from jax import lax
from jax.experimental import pallas as pl
from jax.experimental.pallas import tpu as pltpu
from jax.sharding import PartitionSpec as P

F32, BF16 = jnp.float32, jnp.bfloat16
epsilon = 1e-05
MESH = pl.DeviceIdType.MESH
GROUP = 1
LANES = 128
rows_by_rows = (((0,), (0,)), ((), ()))
cols_by_cols = (((1,), (1,)), ((), ()))


def inverse_rms(values):
    return lax.rsqrt(jnp.mean(values * values, -1, keepdims=True) + epsilon)


def matmul(a, b, dims=(((1,), (0,)), ((), ()))):
    return lax.dot_general(a, b, dims, preferred_element_type=F32)


def kernel(
    sizes,
    tokens, cotangent, ids, probs, gate_hbm, up_hbm, down_hbm,
    grad_gate, grad_up, grad_down,
    w_gate, w_up, w_down, base, select, select_t,
    out_a, out_b, out_r, in_a, in_b, in_r,
    carry_out, carry_in, rows, scaled_rows, work, pre_gate, pre_up,
    all_rows, all_scaled, all_gate, all_up, all_act, spread,
    load_sem, send_a, send_b, send_r, recv_a, recv_b, recv_r,
    send_carry, recv_carry, send_dp, recv_dp,
):
    batches, tokens_b, slots, cap, top, experts, n_dp = sizes
    width = base.shape[-1]
    pieces = width // LANES
    part = width // n_dp
    pairs = tokens_b * top
    section = lax.axis_index("section")
    me = lax.axis_index("expert")
    z = lax.axis_index("dp")

    def expert_at(p):
        return lax.rem(me + p, experts)

    def dp_at(q):
        return lax.rem(z + q, n_dp)

    loads = [
        pltpu.make_async_copy(gate_hbm, w_gate, load_sem.at[0]),
        pltpu.make_async_copy(up_hbm, w_up, load_sem.at[1]),
        pltpu.make_async_copy(down_hbm, w_down, load_sem.at[2]),
    ]

    @pl.when(section == 0)
    def _():
        pltpu.make_async_copy(tokens, base, load_sem.at[3]).start()

    @pl.when(section == 1)
    def _():
        pltpu.make_async_copy(cotangent, base, load_sem.at[3]).start()

    for load in loads:
        load.start()

    barrier = pltpu.get_barrier_semaphore()

    def greet(p, _):
        pl.semaphore_signal(barrier, inc=1, device_id={"expert": expert_at(p)}, device_id_type=MESH)
        return 0

    lax.fori_loop(1, experts, greet, 0)
    for q in range(1, n_dp):
        pl.semaphore_signal(barrier, inc=1, device_id={"dp": dp_at(q)}, device_id_type=MESH)
    pl.semaphore_signal(barrier, inc=1, device_id={"section": 1 - section}, device_id_type=MESH)

    def selectors(b, _):
        own = ids[b]
        order = lax.broadcasted_iota(jnp.int32, (pairs, 1), 0)
        micro = lax.rem(order, tokens_b) // (tokens_b // GROUP)
        order_l = lax.broadcasted_iota(jnp.int32, (pairs, pairs), 1)
        order_s = lax.broadcasted_iota(jnp.int32, (pairs, pairs), 0)
        micro_l = lax.rem(order_l, tokens_b) // (tokens_b // GROUP)
        before = jnp.where((order_l < order_s) & (micro_l == micro), 1.0, 0.0).astype(BF16)
        named = own == lax.broadcasted_iota(jnp.int32, (pairs, experts), 1)
        one_hot = jnp.where(named, 1.0, 0.0)
        earlier = matmul(before, one_hot.astype(BF16))
        rank = jnp.sum(earlier * one_hot, 1, keepdims=True)
        relative = lax.rem(own - me + experts, experts)
        target = (relative * (cap * GROUP) + micro * cap).astype(F32) + rank
        columns = lax.broadcasted_iota(jnp.int32, (pairs, slots), 1).astype(F32)
        select_t[b] = jnp.where(columns == target, 1.0, 0.0).astype(BF16)
        target_row = jnp.sum(jnp.where(order_l == order_s, target, 0.0), 0, keepdims=True)
        lines = lax.broadcasted_iota(jnp.int32, (slots, pairs), 0).astype(F32)
        select[b] = jnp.where(lines == target_row, 1.0, 0.0).astype(BF16)
        return 0

    lax.fori_loop(0, batches, selectors, 0)
    pl.semaphore_wait(barrier, experts - 1 + n_dp - 1 + 1)
    pltpu.make_async_copy(tokens, base, load_sem.at[3]).wait()

    def pack(values, out, own, b):
        for j in range(pieces):
            spread[pl.ds(j, slots, stride=pieces), :] = values[:, j * LANES:(j + 1) * LANES]
        out[b] = spread[...].reshape(slots, pieces, LANES).astype(BF16)
        own[b, 0:cap * GROUP] = out[b, 0:cap * GROUP]

    def unpack(tiles):
        spread[...] = tiles.astype(F32).reshape(slots * pieces, LANES)
        return [
            spread[pl.ds(j, slots, stride=pieces), :].astype(BF16) for j in range(pieces)
        ]

    def put(columns, ref, b):
        for j, column in enumerate(columns):
            ref[b, :, j * LANES:(j + 1) * LANES] = column

    chunk = cap * GROUP

    def exchange(out, into, send_sem, recv_sem, b, sign):
        def one(p, _):
            place = pl.ds(p * chunk, chunk)
            to = lax.rem(me + sign * p + experts, experts)
            pltpu.make_async_remote_copy(
                src_ref=out.at[b, place], dst_ref=into.at[b, place],
                send_sem=send_sem.at[b], recv_sem=recv_sem.at[b],
                device_id={"expert": to}, device_id_type=MESH,
            ).start()
            return 0

        lax.fori_loop(1, experts, one, 0)

    def exchanged(out, into, send_sem, recv_sem, b):
        others = pl.ds(chunk, slots - chunk)
        return pltpu.make_async_remote_copy(
            src_ref=out.at[b, others], dst_ref=into.at[b, others],
            send_sem=send_sem.at[b], recv_sem=recv_sem.at[b],
            device_id={"expert": expert_at(1)}, device_id_type=MESH,
        )

    def carry(b):
        return pltpu.make_async_remote_copy(
            src_ref=carry_out.at[b], dst_ref=carry_in.at[b],
            send_sem=send_carry.at[b], recv_sem=recv_carry.at[b],
            device_id={"section": 1 - section}, device_id_type=MESH,
        )

    def share(source, into, which, b, sliced):
        for q in range(1, n_dp):
            if sliced:
                lanes = pl.ds(pl.multiple_of(dp_at(q) * part, part), part)
                src = source.at[b, :, lanes]
            else:
                src = source.at[0, b]
            pltpu.make_async_remote_copy(
                src_ref=src, dst_ref=into.at[q, b],
                send_sem=send_dp.at[which], recv_sem=recv_dp.at[which],
                device_id={"dp": dp_at(q)}, device_id_type=MESH,
            ).start()

    def shared(into, which):
        others = into.at[pl.ds(1, n_dp - 1)]
        return pltpu.make_async_remote_copy(
            src_ref=others, dst_ref=others,
            send_sem=send_dp.at[which], recv_sem=recv_dp.at[which],
            device_id={"dp": dp_at(1)}, device_id_type=MESH,
        )

    mine = pl.ds(pl.multiple_of(z * part, part), part)

    def dispatch_rows(b, current):
        normed = (current * inverse_rms(current)).astype(BF16)
        chosen = select[b, :, 0:tokens_b] + select[b, :, tokens_b:pairs]
        pack(matmul(chosen, normed), out_a, in_a, b)
        exchange(out_a, in_a, send_a, recv_a, b, 1)

    def dispatch_scaled(b, upstream):
        weights = probs[b]
        scaled = jnp.concatenate(
            [(weights[k * tokens_b:(k + 1) * tokens_b] * upstream).astype(BF16) for k in range(top)], 0
        )
        pack(matmul(select[b], scaled), out_b, in_b, b)
        exchange(out_b, in_b, send_b, recv_b, b, 1)

    def take_rows(b):
        exchanged(out_a, in_a, send_a, recv_a, b).wait_recv()
        put(unpack(in_a[b]), rows, b)
        all_rows[0, b] = rows[b, :, mine]
        share(rows, all_rows, 0, b, True)

    def take_scaled(b):
        exchanged(out_b, in_b, send_b, recv_b, b).wait_recv()
        put(unpack(in_b[b]), scaled_rows, b)
        all_scaled[0, b] = scaled_rows[b, :, mine]
        share(scaled_rows, all_scaled, 1, b, True)

    def hidden(b):
        g = matmul(rows[b], w_gate[...])
        u = matmul(rows[b], w_up[...])
        pre_gate[b] = g
        pre_up[b] = u
        all_act[0, b] = (g * jax.nn.sigmoid(g) * u).astype(BF16)
        share(all_act, all_act, 2, b, False)

    def produce(b):
        pack(matmul(all_act[0, b], w_down[...]), out_r, in_r, b)
        exchange(out_r, in_r, send_r, recv_r, b, -1)

    def hidden_back(b):
        back = matmul(scaled_rows[b], w_down[...], cols_by_cols)
        g, u = pre_gate[b], pre_up[b]
        sg = jax.nn.sigmoid(g)
        all_gate[0, b] = (back * u * sg * (1.0 + g * (1.0 - sg))).astype(BF16)
        all_up[0, b] = (back * (g * sg)).astype(BF16)
        share(all_gate, all_gate, 3, b, False)
        share(all_up, all_up, 4, b, False)

    def produce_back(b):
        pack(
            matmul(all_gate[0, b], w_gate[...], cols_by_cols)
            + matmul(all_up[0, b], w_up[...], cols_by_cols),
            out_r, in_r, b,
        )
        exchange(out_r, in_r, send_r, recv_r, b, -1)

    def take_returned(b):
        exchanged(out_r, in_r, send_r, recv_r, b).wait_recv()
        for j, column in enumerate(unpack(in_r[b])):
            work[:, j * LANES:(j + 1) * LANES] = column
        return matmul(select_t[b], work[...])

    def combine(b):
        chosen = take_returned(b)
        weights = probs[b]
        total = weights[0:tokens_b] * chosen[0:tokens_b]
        for k in range(1, top):
            part_k = slice(k * tokens_b, (k + 1) * tokens_b)
            total = total + weights[part_k] * chosen[part_k]
        carry_out[b] = (base[b].astype(F32) + total).astype(BF16)
        carry(b).start()

    def combine_back(b):
        chosen = take_returned(b)
        d_normed = chosen[0:tokens_b]
        for k in range(1, top):
            d_normed = d_normed + chosen[k * tokens_b:(k + 1) * tokens_b]
        current = carry_in[b].astype(F32)
        scale = inverse_rms(current)
        back = scale * d_normed - current * (scale * scale * scale) * jnp.mean(
            d_normed * current, -1, keepdims=True
        )
        carry_out[b] = (base[b].astype(F32) + back).astype(BF16)
        carry(b).start()

    def wait_loads():
        for load in loads:
            load.wait()

    def loop(count, body):
        def step(i, _):
            body(i)
            return 0

        lax.fori_loop(0, count, step, 0)

    @pl.when(section == 0)
    def _():
        loop(batches, lambda b: dispatch_rows(b, base[b].astype(F32)))
        wait_loads()

        def forward(i):
            @pl.when(i < batches)
            def _():
                take_rows(i)
                hidden(i)
                produce(i)

            @pl.when(i >= 1)
            def _():
                combine(i - 1)

        loop(batches + 1, forward)

        def backward(i):
            @pl.when(i < batches)
            def _():
                carry(i).wait_recv()
                dispatch_scaled(i, carry_in[i].astype(F32))

            @pl.when(i >= 1)
            def _():
                take_scaled(i - 1)
                hidden_back(i - 1)

        loop(batches + 1, backward)

    @pl.when(section == 1)
    def _():
        loop(batches, lambda b: dispatch_scaled(b, base[b].astype(F32)))
        wait_loads()
        loop(batches, take_scaled)

        def both(i):
            @pl.when(i < batches)
            def _():
                carry(i).wait_recv()
                dispatch_rows(i, carry_in[i].astype(F32))

            @pl.when((i >= 1) & (i < batches + 1))
            def _():
                take_rows(i - 1)
                hidden(i - 1)
                hidden_back(i - 1)
                produce_back(i - 1)

            @pl.when(i >= 2)
            def _():
                combine_back(i - 2)

        loop(batches + 2, both)

    shared(all_rows, 0).wait_recv()
    shared(all_scaled, 1).wait_recv()
    shared(all_act, 2).wait_recv()
    shared(all_gate, 3).wait_recv()
    shared(all_up, 4).wait_recv()

    def add_up(q):
        def flat(ref):
            return ref[q].reshape(batches * slots, ref.shape[-1])

        gate_part = matmul(flat(all_rows), flat(all_gate), rows_by_rows)
        up_part = matmul(flat(all_rows), flat(all_up), rows_by_rows)
        down_part = matmul(flat(all_act), flat(all_scaled), rows_by_rows)

        @pl.when(q == 0)
        def _():
            grad_gate[...] = gate_part
            grad_up[...] = up_part
            grad_down[...] = down_part

        @pl.when(q > 0)
        def _():
            grad_gate[...] += gate_part
            grad_up[...] += up_part
            grad_down[...] += down_part

    loop(n_dp, add_up)

    def sent(b):
        exchanged(out_a, in_a, send_a, recv_a, b).wait_send()
        exchanged(out_b, in_b, send_b, recv_b, b).wait_send()
        exchanged(out_r, in_r, send_r, recv_r, b).wait_send()
        carry(b).wait_send()

    loop(batches, sent)
    shared(all_rows, 0).wait_send()
    shared(all_scaled, 1).wait_send()
    shared(all_act, 2).wait_send()
    shared(all_gate, 3).wait_send()
    shared(all_up, 4).wait_send()


def shards(tokens, routes, gate_probs, w_gate, w_up, w_down, cotangent):
    micro_count, row_count, width = tokens.shape
    top = routes.shape[-1]
    experts = lax.axis_size("expert")
    n_dp = lax.axis_size("dp")
    cap = min(row_count, row_count * top // experts + 1)
    hidden = w_gate.shape[-1]
    batches = micro_count // GROUP
    tokens_b = row_count * GROUP
    slots = experts * cap * GROUP
    pieces = width // LANES
    part = width // n_dp

    def columns(array):
        return array[0].reshape(batches, tokens_b, top).transpose(0, 2, 1).reshape(batches, tokens_b * top, 1)

    any_ = pl.BlockSpec(memory_space=pl.ANY)
    vmem = pl.BlockSpec(memory_space=pltpu.VMEM)
    dma = pltpu.SemaphoreType.DMA
    outs = pl.pallas_call(
        functools.partial(kernel, (batches, tokens_b, slots, cap, top, experts, n_dp)),
        out_shape=[
            jax.ShapeDtypeStruct((part, hidden), F32),
            jax.ShapeDtypeStruct((part, hidden), F32),
            jax.ShapeDtypeStruct((hidden, part), F32),
        ],
        in_specs=[any_, any_, vmem, vmem, any_, any_, any_],
        out_specs=[vmem] * 3,
        scratch_shapes=[
            pltpu.VMEM((width, hidden), BF16),
            pltpu.VMEM((width, hidden), BF16),
            pltpu.VMEM((hidden, width), BF16),
            pltpu.VMEM((batches, tokens_b, width), BF16),
            pltpu.VMEM((batches, slots, tokens_b * top), BF16),
            pltpu.VMEM((batches, tokens_b * top, slots), BF16),
            *[pltpu.VMEM((batches, slots, pieces, LANES), BF16)] * 6,
            *[pltpu.VMEM((batches, tokens_b, width), BF16)] * 2,
            *[pltpu.VMEM((batches, slots, width), BF16)] * 2,
            pltpu.VMEM((slots, width), BF16),
            *[pltpu.VMEM((batches, slots, hidden), F32)] * 2,
            *[pltpu.VMEM((n_dp, batches, slots, part), BF16)] * 2,
            *[pltpu.VMEM((n_dp, batches, slots, hidden), BF16)] * 3,
            pltpu.VMEM((slots * pieces, LANES), F32),
            dma((4,)),
            *[dma((batches,))] * 6,
            *[dma((batches,))] * 2,
            *[dma((5,))] * 2,
        ],
        compiler_params=pltpu.CompilerParams(
            collective_id=0, has_side_effects=True, vmem_limit_bytes=60 * 1024 * 1024
        ),
    )(
        tokens, cotangent, columns(routes), columns(gate_probs),
        w_gate[0, 0], w_up[0, 0], w_down[0, 0],
    )
    return tuple(out[None, None] for out in outs)


def solution(mesh):
    in_specs = (
        P(None, ("expert", "dp"), None),
        P("section", None, ("expert", "dp"), None),
        P("section", None, ("expert", "dp"), None),
        P("section", "expert", None, None),
        P("section", "expert", None, None),
        P("section", "expert", None, None),
        P(None, ("expert", "dp"), None),
    )
    out_specs = (
        P("section", "expert", "dp", None),
        P("section", "expert", "dp", None),
        P("section", "expert", None, "dp"),
    )
    return jax.shard_map(shards, mesh=mesh, in_specs=in_specs, out_specs=out_specs, check_vma=False)
```

```python
import functools
import jax
import jax.numpy as jnp
from jax import lax
from jax.experimental import pallas as pl
from jax.experimental.pallas import tpu as pltpu
from jax.sharding import PartitionSpec as P

F32, BF16 = jnp.float32, jnp.bfloat16
epsilon = 1e-05
MESH = pl.DeviceIdType.MESH
LANES = 128
rows_by_rows = (((0,), (0,)), ((), ()))
cols_by_cols = (((1,), (1,)), ((), ()))


def inverse_rms(values):
    return lax.rsqrt(jnp.mean(values * values, -1, keepdims=True) + epsilon)


def matmul(a, b, dims=(((1,), (0,)), ((), ()))):
    return lax.dot_general(a, b, dims, preferred_element_type=F32)


def kernel(
    sizes,
    tokens, cotangent, ids, probs, gate_hbm, up_hbm, down_hbm,
    grad_gate, grad_up, grad_down,
    w_gate, w_up, w_down, base, select, select_t, weights,
    out_a, out_b, out_r, in_a, in_b, in_r,
    carry_out, carry_in, rows, scaled_rows, work, pre_gate, pre_up,
    all_rows, all_scaled, all_gate, all_up, all_act, spread,
    load_sem, send_a, send_b, send_r, recv_a, recv_b, recv_r,
    send_carry, recv_carry, send_dp, recv_dp,
):
    batches, tokens_b, slots, cap, top, experts, n_dp = sizes
    width = base.shape[-1]
    pieces = width // LANES
    part = width // n_dp
    pairs = tokens_b * top
    section = lax.axis_index("section")
    me = lax.axis_index("expert")
    z = lax.axis_index("dp")

    def expert_at(p):
        return lax.rem(me + p, experts)

    def dp_at(q):
        return lax.rem(z + q, n_dp)

    loads = [
        pltpu.make_async_copy(gate_hbm, w_gate, load_sem.at[0]),
        pltpu.make_async_copy(up_hbm, w_up, load_sem.at[1]),
        pltpu.make_async_copy(down_hbm, w_down, load_sem.at[2]),
    ]

    @pl.when(section == 0)
    def _():
        pltpu.make_async_copy(tokens, base, load_sem.at[3]).start()

    @pl.when(section == 1)
    def _():
        pltpu.make_async_copy(cotangent, base, load_sem.at[3]).start()

    for load in loads:
        load.start()

    barrier = pltpu.get_barrier_semaphore()

    def greet(p, _):
        pl.semaphore_signal(barrier, inc=1, device_id={"expert": expert_at(p)}, device_id_type=MESH)
        return 0

    lax.fori_loop(1, experts, greet, 0)
    for q in range(1, n_dp):
        pl.semaphore_signal(barrier, inc=1, device_id={"dp": dp_at(q)}, device_id_type=MESH)
    pl.semaphore_signal(barrier, inc=1, device_id={"section": 1 - section}, device_id_type=MESH)

    def upright(row):
        size = row.shape[-1]
        along = lax.broadcasted_iota(jnp.int32, (size, size), 1)
        down = lax.broadcasted_iota(jnp.int32, (size, size), 0)
        return jnp.sum(jnp.where(along == down, row, 0.0), 1, keepdims=True)

    def selectors(b, _):
        named_row = ids[b].astype(F32)
        prob_row = probs[b]
        own = jnp.concatenate([upright(named_row[k:k + 1]) for k in range(top)], 0)
        weights[b] = jnp.concatenate([upright(prob_row[k:k + 1]) for k in range(top)], 0)
        own = own.astype(jnp.int32)
        order_l = lax.broadcasted_iota(jnp.int32, (pairs, pairs), 1)
        order_s = lax.broadcasted_iota(jnp.int32, (pairs, pairs), 0)
        before = jnp.where(order_l < order_s, 1.0, 0.0).astype(BF16)
        named = own == lax.broadcasted_iota(jnp.int32, (pairs, experts), 1)
        one_hot = jnp.where(named, 1.0, 0.0)
        earlier = matmul(before, one_hot.astype(BF16))
        rank = jnp.sum(earlier * one_hot, 1, keepdims=True)
        relative = own - me
        relative = jnp.where(relative < 0, relative + experts, relative)
        target = (relative * cap).astype(F32) + rank
        columns = lax.broadcasted_iota(jnp.int32, (pairs, slots), 1).astype(F32)
        select_t[b] = jnp.where(columns == target, 1.0, 0.0).astype(BF16)
        target_row = jnp.sum(jnp.where(order_l == order_s, target, 0.0), 0, keepdims=True)
        lines = lax.broadcasted_iota(jnp.int32, (slots, pairs), 0).astype(F32)
        select[b] = jnp.where(lines == target_row, 1.0, 0.0).astype(BF16)
        return 0

    lax.fori_loop(0, batches, selectors, 0)
    pl.semaphore_wait(barrier, experts - 1 + n_dp - 1 + 1)
    pltpu.make_async_copy(tokens, base, load_sem.at[3]).wait()

    def pack(values, out, own, b):
        for j in range(pieces):
            spread[pl.ds(j, slots, stride=pieces), :] = values[:, j * LANES:(j + 1) * LANES]
        out[b] = spread[...].reshape(slots, pieces, LANES).astype(BF16)
        own[b, 0:cap] = out[b, 0:cap]

    def unpack(tiles):
        spread[...] = tiles.astype(F32).reshape(slots * pieces, LANES)
        return [
            spread[pl.ds(j, slots, stride=pieces), :].astype(BF16) for j in range(pieces)
        ]

    def put(columns, ref, b):
        for j, column in enumerate(columns):
            ref[b, :, j * LANES:(j + 1) * LANES] = column

    chunk = cap

    def exchange(out, into, send_sem, recv_sem, b, sign):
        def one(p, _):
            place = pl.ds(p * chunk, chunk)
            to = lax.rem(me + sign * p + experts, experts)
            pltpu.make_async_remote_copy(
                src_ref=out.at[b, place], dst_ref=into.at[b, place],
                send_sem=send_sem.at[b], recv_sem=recv_sem.at[b],
                device_id={"expert": to}, device_id_type=MESH,
            ).start()
            return 0

        lax.fori_loop(1, experts, one, 0)

    def exchanged(out, into, send_sem, recv_sem, b):
        others = pl.ds(chunk, slots - chunk)
        return pltpu.make_async_remote_copy(
            src_ref=out.at[b, others], dst_ref=into.at[b, others],
            send_sem=send_sem.at[b], recv_sem=recv_sem.at[b],
            device_id={"expert": expert_at(1)}, device_id_type=MESH,
        )

    def carry(b):
        return pltpu.make_async_remote_copy(
            src_ref=carry_out.at[b], dst_ref=carry_in.at[b],
            send_sem=send_carry.at[b], recv_sem=recv_carry.at[b],
            device_id={"section": 1 - section}, device_id_type=MESH,
        )

    def to_dp(src, into, which, b, q, to):
        return pltpu.make_async_remote_copy(
            src_ref=src, dst_ref=into.at[b, q],
            send_sem=send_dp.at[which], recv_sem=recv_dp.at[which, q, b],
            device_id={"dp": to}, device_id_type=MESH,
        )

    def share_part(source, into, which, b):
        for q in range(1, n_dp):
            lanes = pl.ds(pl.multiple_of(dp_at(q) * part, part), part)
            to_dp(source.at[b, :, lanes], into, which, b, q, dp_at(q)).start()

    def share(into, which, b):
        for q in (1, n_dp - 1):
            to_dp(into.at[b, 0], into, which, b, q, dp_at(q)).start()

    def arrived(into, which, b, q):
        to_dp(into.at[b, q], into, which, b, q, dp_at(1)).wait_recv()

    def forward(into, which, b, q):
        arrived(into, which, b, q)
        to_dp(into.at[b, q], into, which, b, 2, dp_at(q)).start()

    def left(into, which):
        others = into.at[:, pl.ds(1, n_dp - 1)]
        pltpu.make_async_remote_copy(
            src_ref=others, dst_ref=others,
            send_sem=send_dp.at[which], recv_sem=recv_dp.at[which, 0, 0],
            device_id={"dp": dp_at(1)}, device_id_type=MESH,
        ).wait_send()

    mine = pl.ds(pl.multiple_of(z * part, part), part)

    def dispatch_rows(b, current):
        normed = (current * inverse_rms(current)).astype(BF16)
        chosen = select[b, :, 0:tokens_b] + select[b, :, tokens_b:pairs]
        pack(matmul(chosen, normed), out_a, in_a, b)
        exchange(out_a, in_a, send_a, recv_a, b, 1)

    def dispatch_scaled(b, upstream):
        scaled = jnp.concatenate(
            [(weights[b, k * tokens_b:(k + 1) * tokens_b] * upstream).astype(BF16) for k in range(top)], 0
        )
        pack(matmul(select[b], scaled), out_b, in_b, b)
        exchange(out_b, in_b, send_b, recv_b, b, 1)

    def take_rows(b):
        exchanged(out_a, in_a, send_a, recv_a, b).wait_recv()
        put(unpack(in_a[b]), rows, b)
        all_rows[b, 0] = rows[b, :, mine]
        share_part(rows, all_rows, 0, b)

    def take_scaled(b):
        exchanged(out_b, in_b, send_b, recv_b, b).wait_recv()
        put(unpack(in_b[b]), scaled_rows, b)
        all_scaled[b, 0] = scaled_rows[b, :, mine]
        share_part(scaled_rows, all_scaled, 1, b)

    def hidden(b):
        g = matmul(rows[b], w_gate[...])
        u = matmul(rows[b], w_up[...])
        pre_gate[b] = g
        pre_up[b] = u
        all_act[b, 0] = (g * jax.nn.sigmoid(g) * u).astype(BF16)
        share(all_act, 2, b)

    def produce(b):
        pack(matmul(all_act[b, 0], w_down[...]), out_r, in_r, b)
        exchange(out_r, in_r, send_r, recv_r, b, -1)

    def hidden_back(b):
        back = matmul(scaled_rows[b], w_down[...], cols_by_cols)
        g, u = pre_gate[b], pre_up[b]
        sg = jax.nn.sigmoid(g)
        all_gate[b, 0] = (back * u * sg * (1.0 + g * (1.0 - sg))).astype(BF16)
        all_up[b, 0] = (back * (g * sg)).astype(BF16)
        share(all_gate, 3, b)
        share(all_up, 4, b)

    def produce_back(b):
        pack(
            matmul(all_gate[b, 0], w_gate[...], cols_by_cols)
            + matmul(all_up[b, 0], w_up[...], cols_by_cols),
            out_r, in_r, b,
        )
        exchange(out_r, in_r, send_r, recv_r, b, -1)

    def take_returned(b):
        exchanged(out_r, in_r, send_r, recv_r, b).wait_recv()
        for j, column in enumerate(unpack(in_r[b])):
            work[:, j * LANES:(j + 1) * LANES] = column
        return matmul(select_t[b], work[...])

    def combine(b):
        chosen = take_returned(b)
        total = weights[b, 0:tokens_b] * chosen[0:tokens_b]
        for k in range(1, top):
            part_k = slice(k * tokens_b, (k + 1) * tokens_b)
            total = total + weights[b, part_k] * chosen[part_k]
        carry_out[b] = (base[b].astype(F32) + total).astype(BF16)
        carry(b).start()

    def combine_back(b):
        chosen = take_returned(b)
        d_normed = chosen[0:tokens_b]
        for k in range(1, top):
            d_normed = d_normed + chosen[k * tokens_b:(k + 1) * tokens_b]
        current = carry_in[b].astype(F32)
        scale = inverse_rms(current)
        back = scale * d_normed - current * (scale * scale * scale) * jnp.mean(
            d_normed * current, -1, keepdims=True
        )
        carry_out[b] = (base[b].astype(F32) + back).astype(BF16)
        carry(b).start()

    def forward_act(b):
        @pl.when(lax.rem(b, 2) == 0)
        def _():
            forward(all_act, 2, b, 1)

        @pl.when(lax.rem(b, 2) == 1)
        def _():
            forward(all_act, 2, b, n_dp - 1)

    def forward_back(b):
        forward(all_gate, 3, b, 1)
        forward(all_up, 4, b, n_dp - 1)

    def all_arrived(b):
        for q in range(1, n_dp):
            arrived(all_rows, 0, b, q)
            arrived(all_scaled, 1, b, q)

        @pl.when(lax.rem(b, 2) == 0)
        def _():
            arrived(all_act, 2, b, n_dp - 1)

        @pl.when(lax.rem(b, 2) == 1)
        def _():
            arrived(all_act, 2, b, 1)

        arrived(all_gate, 3, b, n_dp - 1)
        arrived(all_up, 4, b, 1)
        for which, into in ((2, all_act), (3, all_gate), (4, all_up)):
            arrived(into, which, b, 2)

    def wait_loads():
        for load in loads:
            load.wait()

    def loop(count, body):
        def step(i, _):
            body(i)
            return 0

        lax.fori_loop(0, count, step, 0)

    @pl.when(section == 0)
    def _():
        loop(batches, lambda b: dispatch_rows(b, base[b].astype(F32)))
        wait_loads()

        def forward(i):
            @pl.when(i < batches)
            def _():
                take_rows(i)
                hidden(i)
                produce(i)

            @pl.when(i >= 1)
            def _():
                combine(i - 1)

        loop(batches + 1, forward)

        def backward(i):
            @pl.when(i < batches)
            def _():
                carry(i).wait_recv()
                dispatch_scaled(i, carry_in[i].astype(F32))
                forward_act(i)

            @pl.when(i >= 1)
            def _():
                take_scaled(i - 1)
                hidden_back(i - 1)

        loop(batches + 1, backward)

    @pl.when(section == 1)
    def _():
        loop(batches, lambda b: dispatch_scaled(b, base[b].astype(F32)))
        wait_loads()
        loop(batches, take_scaled)

        def both(i):
            @pl.when(i < batches)
            def _():
                carry(i).wait_recv()
                dispatch_rows(i, carry_in[i].astype(F32))

            @pl.when((i >= 1) & (i < batches + 1))
            def _():
                take_rows(i - 1)
                hidden(i - 1)
                hidden_back(i - 1)
                produce_back(i - 1)

            @pl.when(i >= 2)
            def _():
                combine_back(i - 2)

        loop(batches + 2, both)
        loop(batches, forward_act)

    loop(batches, forward_back)

    def add_up(b):
        all_arrived(b)

        def flat(ref):
            return ref[b].reshape(n_dp * slots, ref.shape[-1])

        gate_part = matmul(flat(all_rows), flat(all_gate), rows_by_rows)
        up_part = matmul(flat(all_rows), flat(all_up), rows_by_rows)
        down_part = matmul(flat(all_act), flat(all_scaled), rows_by_rows)

        @pl.when(b == 0)
        def _():
            grad_gate[...] = gate_part
            grad_up[...] = up_part
            grad_down[...] = down_part

        @pl.when(b > 0)
        def _():
            grad_gate[...] += gate_part
            grad_up[...] += up_part
            grad_down[...] += down_part

    loop(batches, add_up)

    def sent(b):
        exchanged(out_a, in_a, send_a, recv_a, b).wait_send()
        exchanged(out_b, in_b, send_b, recv_b, b).wait_send()
        exchanged(out_r, in_r, send_r, recv_r, b).wait_send()
        carry(b).wait_send()

    loop(batches, sent)
    left(all_rows, 0)
    left(all_scaled, 1)
    left(all_act, 2)
    left(all_gate, 3)
    left(all_up, 4)


def shards(tokens, routes, gate_probs, w_gate, w_up, w_down, cotangent):
    micro_count, row_count, width = tokens.shape
    top = routes.shape[-1]
    experts = lax.axis_size("expert")
    n_dp = lax.axis_size("dp")
    cap = min(row_count, row_count * top // experts + 1)
    hidden = w_gate.shape[-1]
    batches, tokens_b = micro_count, row_count
    slots = experts * cap
    pieces = width // LANES
    part = width // n_dp

    def in_hbm(array):
        return pltpu.with_memory_space_constraint(array, pltpu.HBM)

    any_ = pl.BlockSpec(memory_space=pl.ANY)
    vmem = pl.BlockSpec(memory_space=pltpu.VMEM)
    dma = pltpu.SemaphoreType.DMA
    outs = pl.pallas_call(
        functools.partial(kernel, (batches, tokens_b, slots, cap, top, experts, n_dp)),
        out_shape=[
            jax.ShapeDtypeStruct((part, hidden), F32),
            jax.ShapeDtypeStruct((part, hidden), F32),
            jax.ShapeDtypeStruct((hidden, part), F32),
        ],
        in_specs=[any_, any_, vmem, vmem, any_, any_, any_],
        out_specs=[vmem] * 3,
        scratch_shapes=[
            pltpu.VMEM((width, hidden), BF16),
            pltpu.VMEM((width, hidden), BF16),
            pltpu.VMEM((hidden, width), BF16),
            pltpu.VMEM((batches, tokens_b, width), BF16),
            pltpu.VMEM((batches, slots, tokens_b * top), BF16),
            pltpu.VMEM((batches, tokens_b * top, slots), BF16),
            pltpu.VMEM((batches, tokens_b * top, 1), F32),
            *[pltpu.VMEM((batches, slots, pieces, LANES), BF16)] * 6,
            *[pltpu.VMEM((batches, tokens_b, width), BF16)] * 2,
            *[pltpu.VMEM((batches, slots, width), BF16)] * 2,
            pltpu.VMEM((slots, width), BF16),
            *[pltpu.VMEM((batches, slots, hidden), F32)] * 2,
            *[pltpu.VMEM((batches, n_dp, slots, part), BF16)] * 2,
            *[pltpu.VMEM((batches, n_dp, slots, hidden), BF16)] * 3,
            pltpu.VMEM((slots * pieces, LANES), F32),
            dma((4,)),
            *[dma((batches,))] * 6,
            *[dma((batches,))] * 2,
            dma((5,)),
            dma((5, n_dp, batches)),
        ],
        compiler_params=pltpu.CompilerParams(
            collective_id=0, has_side_effects=True, vmem_limit_bytes=38 * 1024 * 1024
        ),
    )(
        in_hbm(tokens), in_hbm(cotangent), routes[0].transpose(0, 2, 1), gate_probs[0].transpose(0, 2, 1),
        in_hbm(w_gate[0, 0]), in_hbm(w_up[0, 0]), in_hbm(w_down[0, 0]),
    )
    return tuple(out[None, None] for out in outs)


def solution(mesh):
    in_specs = (
        P(None, ("expert", "dp"), None),
        P("section", None, ("expert", "dp"), None),
        P("section", None, ("expert", "dp"), None),
        P("section", "expert", None, None),
        P("section", "expert", None, None),
        P("section", "expert", None, None),
        P(None, ("expert", "dp"), None),
    )
    out_specs = (
        P("section", "expert", "dp", None),
        P("section", "expert", "dp", None),
        P("section", "expert", None, "dp"),
    )
    return jax.shard_map(shards, mesh=mesh, in_specs=in_specs, out_specs=out_specs, check_vma=False)
```

```python
import functools
import jax
import jax.numpy as jnp
from jax import lax
from jax.experimental import pallas as pl
from jax.experimental.pallas import tpu as pltpu
from jax.sharding import PartitionSpec as P

F32, BF16 = jnp.float32, jnp.bfloat16
epsilon = 1e-05
MESH = pl.DeviceIdType.MESH
LANES = 128
rows_by_rows = (((0,), (0,)), ((), ()))
cols_by_cols = (((1,), (1,)), ((), ()))


def inverse_rms(values):
    return lax.rsqrt(jnp.mean(values * values, -1, keepdims=True) + epsilon)


def matmul(a, b, dims=(((1,), (0,)), ((), ()))):
    return lax.dot_general(a, b, dims, preferred_element_type=F32)


def kernel(
    sizes,
    tokens, cotangent, ids_hbm, probs_hbm, gate_hbm, up_hbm, down_hbm,
    grad_gate, grad_up, grad_down,
    ids, probs, w_hidden, w_down, w_hidden_t, w_down_t, base, select, select_t, weights,
    out_a, out_b, out_r, in_a, in_b, in_r,
    carry_out, carry_in, rows, scaled_rows, work, pre_hidden,
    all_rows, all_scaled, all_back, all_act, spread,
    load_sem, send_a, send_b, send_r, recv_a, recv_b, recv_r,
    send_carry, recv_carry, send_dp, recv_dp,
):
    batches, tokens_b, slots, cap, top, experts, n_dp = sizes
    width = base.shape[-1]
    units = w_down.shape[0]
    pieces = width // LANES
    part = width // n_dp
    pairs = tokens_b * top
    section = lax.axis_index("section")
    me = lax.axis_index("expert")
    z = lax.axis_index("dp")

    def expert_at(p):
        return lax.rem(me + p, experts)

    def dp_at(q):
        return lax.rem(z + q, n_dp)

    loads = [
        pltpu.make_async_copy(gate_hbm, w_hidden.at[:, pl.ds(0, units)], load_sem.at[0]),
        pltpu.make_async_copy(up_hbm, w_hidden.at[:, pl.ds(units, units)], load_sem.at[1]),
        pltpu.make_async_copy(down_hbm, w_down, load_sem.at[2]),
    ]

    @pl.when(section == 0)
    def _():
        pltpu.make_async_copy(tokens, base, load_sem.at[3]).start()

    @pl.when(section == 1)
    def _():
        pltpu.make_async_copy(cotangent, base, load_sem.at[3]).start()

    tables = [
        pltpu.make_async_copy(ids_hbm, ids, load_sem.at[4]),
        pltpu.make_async_copy(probs_hbm, probs, load_sem.at[5]),
    ]
    for load in tables + loads:
        load.start()

    barrier = pltpu.get_barrier_semaphore()

    def greet(p, _):
        pl.semaphore_signal(barrier, inc=1, device_id={"expert": expert_at(p)}, device_id_type=MESH)
        return 0

    lax.fori_loop(1, experts, greet, 0)
    for q in range(1, n_dp):
        pl.semaphore_signal(barrier, inc=1, device_id={"dp": dp_at(q)}, device_id_type=MESH)
    pl.semaphore_signal(barrier, inc=1, device_id={"section": 1 - section}, device_id_type=MESH)

    def upright(row):
        size = row.shape[-1]
        along = lax.broadcasted_iota(jnp.int32, (size, size), 1)
        down = lax.broadcasted_iota(jnp.int32, (size, size), 0)
        return jnp.sum(jnp.where(along == down, row, 0.0), 1, keepdims=True)

    def selectors(b):
        named_row = ids[b].astype(F32)
        prob_row = probs[b]
        own = jnp.concatenate([upright(named_row[k:k + 1]) for k in range(top)], 0)
        weights[b] = jnp.concatenate([upright(prob_row[k:k + 1]) for k in range(top)], 0)
        own = own.astype(jnp.int32)
        order_l = lax.broadcasted_iota(jnp.int32, (pairs, pairs), 1)
        order_s = lax.broadcasted_iota(jnp.int32, (pairs, pairs), 0)
        before = jnp.where(order_l < order_s, 1.0, 0.0).astype(BF16)
        named = own == lax.broadcasted_iota(jnp.int32, (pairs, experts), 1)
        one_hot = jnp.where(named, 1.0, 0.0)
        earlier = matmul(before, one_hot.astype(BF16))
        rank = jnp.sum(earlier * one_hot, 1, keepdims=True)
        relative = own - me
        relative = jnp.where(relative < 0, relative + experts, relative)
        target = (relative * cap).astype(F32) + rank
        columns = lax.broadcasted_iota(jnp.int32, (pairs, slots), 1).astype(F32)
        select_t[b] = jnp.where(columns == target, 1.0, 0.0).astype(BF16)
        target_row = jnp.sum(jnp.where(order_l == order_s, target, 0.0), 0, keepdims=True)
        lines = lax.broadcasted_iota(jnp.int32, (slots, pairs), 0).astype(F32)
        select[b] = jnp.where(lines == target_row, 1.0, 0.0).astype(BF16)

    for load in tables:
        load.wait()
    pltpu.make_async_copy(tokens, base, load_sem.at[3]).wait()

    def pack(values, out, own, b):
        for j in range(pieces):
            spread[pl.ds(j, slots, stride=pieces), :] = values[:, j * LANES:(j + 1) * LANES]
        out[b] = spread[...].reshape(slots, pieces, LANES).astype(BF16)
        own[b, 0:cap] = out[b, 0:cap]

    def unpack(tiles):
        spread[...] = tiles.astype(F32).reshape(slots * pieces, LANES)
        return [
            spread[pl.ds(j, slots, stride=pieces), :].astype(BF16) for j in range(pieces)
        ]

    def put(columns, ref, b):
        for j, column in enumerate(columns):
            ref[b, :, j * LANES:(j + 1) * LANES] = column

    chunk = cap

    def exchange(out, into, send_sem, recv_sem, b, sign):
        def one(p, _):
            place = pl.ds(p * chunk, chunk)
            to = lax.rem(me + sign * p + experts, experts)
            pltpu.make_async_remote_copy(
                src_ref=out.at[b, place], dst_ref=into.at[b, place],
                send_sem=send_sem.at[b], recv_sem=recv_sem.at[b],
                device_id={"expert": to}, device_id_type=MESH,
            ).start()
            return 0

        lax.fori_loop(1, experts, one, 0)

    def exchanged(out, into, send_sem, recv_sem, b):
        others = pl.ds(chunk, slots - chunk)
        return pltpu.make_async_remote_copy(
            src_ref=out.at[b, others], dst_ref=into.at[b, others],
            send_sem=send_sem.at[b], recv_sem=recv_sem.at[b],
            device_id={"expert": expert_at(1)}, device_id_type=MESH,
        )

    def carry(b):
        return pltpu.make_async_remote_copy(
            src_ref=carry_out.at[b], dst_ref=carry_in.at[b],
            send_sem=send_carry.at[b], recv_sem=recv_carry.at[b],
            device_id={"section": 1 - section}, device_id_type=MESH,
        )

    def to_dp(src, into, which, b, q, to):
        return pltpu.make_async_remote_copy(
            src_ref=src, dst_ref=into.at[b, q],
            send_sem=send_dp.at[which], recv_sem=recv_dp.at[which, q, b],
            device_id={"dp": to}, device_id_type=MESH,
        )

    def share_part(source, into, which, b):
        for q in range(1, n_dp):
            lanes = pl.ds(pl.multiple_of(dp_at(q) * part, part), part)
            to_dp(source.at[b, :, lanes], into, which, b, q, dp_at(q)).start()

    def share(into, which, b):
        for q in (1, n_dp - 1):
            to_dp(into.at[b, 0], into, which, b, q, dp_at(q)).start()

    def arrived(into, which, b, q):
        to_dp(into.at[b, q], into, which, b, q, dp_at(1)).wait_recv()

    def forward(into, which, b, q):
        arrived(into, which, b, q)
        to_dp(into.at[b, q], into, which, b, 2, dp_at(q)).start()

    def left(into, which):
        others = into.at[:, pl.ds(1, n_dp - 1)]
        pltpu.make_async_remote_copy(
            src_ref=others, dst_ref=others,
            send_sem=send_dp.at[which], recv_sem=recv_dp.at[which, 0, 0],
            device_id={"dp": dp_at(1)}, device_id_type=MESH,
        ).wait_send()

    mine = pl.ds(pl.multiple_of(z * part, part), part)

    def pack_rows(b, current):
        normed = (current * inverse_rms(current)).astype(BF16)
        chosen = select[b, :, 0:tokens_b] + select[b, :, tokens_b:pairs]
        pack(matmul(chosen, normed), out_a, in_a, b)

    def dispatch_rows(b, current):
        pack_rows(b, current)
        send_rows(b)

    def send_rows(b):
        exchange(out_a, in_a, send_a, recv_a, b, 1)

    def pack_scaled(b, upstream):
        scaled = jnp.concatenate(
            [(weights[b, k * tokens_b:(k + 1) * tokens_b] * upstream).astype(BF16) for k in range(top)], 0
        )
        pack(matmul(select[b], scaled), out_b, in_b, b)

    def dispatch_scaled(b, upstream):
        pack_scaled(b, upstream)
        send_scaled(b)

    def send_scaled(b):
        exchange(out_b, in_b, send_b, recv_b, b, 1)

    def take_rows(b):
        exchanged(out_a, in_a, send_a, recv_a, b).wait_recv()
        put(unpack(in_a[b]), rows, b)
        all_rows[b, 0] = rows[b, :, mine]
        share_part(rows, all_rows, 0, b)

    def take_scaled(b):
        exchanged(out_b, in_b, send_b, recv_b, b).wait_recv()
        put(unpack(in_b[b]), scaled_rows, b)
        all_scaled[b, 0] = scaled_rows[b, :, mine]
        share_part(scaled_rows, all_scaled, 1, b)

    def hidden(b):
        pre = matmul(rows[b], w_hidden[...])
        pre_hidden[b] = pre
        g, u = pre[:, 0:units], pre[:, units:2 * units]
        all_act[b, 0] = (g * jax.nn.sigmoid(g) * u).astype(BF16)
        share(all_act, 2, b)

    def produce(b):
        pack(matmul(all_act[b, 0], w_down[...]), out_r, in_r, b)
        exchange(out_r, in_r, send_r, recv_r, b, -1)

    def hidden_back(b):
        back = matmul(scaled_rows[b], w_down_t[...])
        g, u = pre_hidden[b, :, 0:units], pre_hidden[b, :, units:2 * units]
        sg = jax.nn.sigmoid(g)
        all_back[b, 0, :, 0:units] = (back * u * sg * (1.0 + g * (1.0 - sg))).astype(BF16)
        all_back[b, 0, :, units:2 * units] = (back * (g * sg)).astype(BF16)
        share(all_back, 3, b)

    def produce_back(b):
        pack(matmul(all_back[b, 0], w_hidden_t[...]), out_r, in_r, b)
        exchange(out_r, in_r, send_r, recv_r, b, -1)

    def turn_down(b):
        place = pl.ds(pl.multiple_of(b * (width // batches), width // batches), width // batches)
        w_down_t[place, :] = w_down[:, place].T

    def turn_hidden(b):
        place = pl.ds(pl.multiple_of(b * (width // batches), width // batches), width // batches)
        w_hidden_t[:, place] = w_hidden[place, :].T

    def take_returned(b):
        exchanged(out_r, in_r, send_r, recv_r, b).wait_recv()
        for j, column in enumerate(unpack(in_r[b])):
            work[:, j * LANES:(j + 1) * LANES] = column
        return matmul(select_t[b], work[...])

    def combine(b):
        chosen = take_returned(b)
        total = weights[b, 0:tokens_b] * chosen[0:tokens_b]
        for k in range(1, top):
            part_k = slice(k * tokens_b, (k + 1) * tokens_b)
            total = total + weights[b, part_k] * chosen[part_k]
        carry_out[b] = (base[b].astype(F32) + total).astype(BF16)
        carry(b).start()

    def combine_back(b):
        chosen = take_returned(b)
        d_normed = chosen[0:tokens_b]
        for k in range(1, top):
            d_normed = d_normed + chosen[k * tokens_b:(k + 1) * tokens_b]
        current = carry_in[b].astype(F32)
        scale = inverse_rms(current)
        back = scale * d_normed - current * (scale * scale * scale) * jnp.mean(
            d_normed * current, -1, keepdims=True
        )
        carry_out[b] = (base[b].astype(F32) + back).astype(BF16)
        carry(b).start()

    def forward_act(b):
        @pl.when(lax.rem(b, 2) == 0)
        def _():
            forward(all_act, 2, b, 1)

        @pl.when(lax.rem(b, 2) == 1)
        def _():
            forward(all_act, 2, b, n_dp - 1)

    def forward_back(b):
        for q, lanes in ((1, pl.ds(0, units)), (n_dp - 1, pl.ds(units, units))):
            arrived(all_back, 3, b, q)
            pltpu.make_async_remote_copy(
                src_ref=all_back.at[b, q, :, lanes], dst_ref=all_back.at[b, 2, :, lanes],
                send_sem=send_dp.at[3], recv_sem=recv_dp.at[3, 2, b],
                device_id={"dp": dp_at(q)}, device_id_type=MESH,
            ).start()

    def all_arrived(b):
        for q in range(1, n_dp):
            arrived(all_rows, 0, b, q)
            arrived(all_scaled, 1, b, q)

        @pl.when(lax.rem(b, 2) == 0)
        def _():
            arrived(all_act, 2, b, n_dp - 1)

        @pl.when(lax.rem(b, 2) == 1)
        def _():
            arrived(all_act, 2, b, 1)

        arrived(all_act, 2, b, 2)
        arrived(all_back, 3, b, 2)

    def wait_loads():
        for load in loads:
            load.wait()

    def loop(count, body, first=0):
        def step(i, _):
            body(i)
            return 0

        lax.fori_loop(first, count, step, 0)

    selectors(0)

    @pl.when(section == 0)
    def _():
        pack_rows(0, base[0].astype(F32))

    @pl.when(section == 1)
    def _():
        pack_scaled(0, base[0].astype(F32))

    pl.semaphore_wait(barrier, experts - 1 + n_dp - 1 + 1)

    @pl.when(section == 0)
    def _():
        def start(b):
            selectors(b)
            dispatch_rows(b, base[b].astype(F32))

        send_rows(0)
        loop(batches, start, 1)
        wait_loads()

        def forward_step(i):
            @pl.when(i < batches)
            def _():
                take_rows(i)
                hidden(i)
                produce(i)

            @pl.when(i >= 1)
            def _():
                combine(i - 1)

        loop(batches + 1, forward_step)
        loop(batches, turn_down)

        def backward(i):
            @pl.when(i < batches)
            def _():
                carry(i).wait_recv()
                dispatch_scaled(i, carry_in[i].astype(F32))
                forward_act(i)

            @pl.when(i >= 1)
            def _():
                take_scaled(i - 1)
                hidden_back(i - 1)

            @pl.when(i >= 2)
            def _():
                forward_back(i - 2)

        loop(batches + 1, backward)

    @pl.when(section == 1)
    def _():
        def start(b):
            selectors(b)
            dispatch_scaled(b, base[b].astype(F32))

        send_scaled(0)
        loop(batches, start, 1)
        wait_loads()

        def prepare(b):
            turn_down(b)
            take_scaled(b)
            turn_hidden(b)

        loop(batches, prepare)

        def both(i):
            @pl.when(i < batches)
            def _():
                carry(i).wait_recv()
                dispatch_rows(i, carry_in[i].astype(F32))

            @pl.when((i >= 1) & (i < batches + 1))
            def _():
                take_rows(i - 1)
                hidden(i - 1)
                hidden_back(i - 1)
                produce_back(i - 1)

            @pl.when(i >= 2)
            def _():
                combine_back(i - 2)
                forward_act(i - 2)
                forward_back(i - 2)

        loop(batches + 2, both)

    def add_up(b):
        all_arrived(b)

        def flat(ref):
            return ref[b].reshape(n_dp * slots, ref.shape[-1])

        both = matmul(flat(all_rows), flat(all_back), rows_by_rows)
        gate_part, up_part = both[:, 0:units], both[:, units:2 * units]
        down_part = matmul(flat(all_act), flat(all_scaled), rows_by_rows)

        @pl.when(b == 0)
        def _():
            grad_gate[...] = gate_part
            grad_up[...] = up_part
            grad_down[...] = down_part

        @pl.when(b > 0)
        def _():
            grad_gate[...] += gate_part
            grad_up[...] += up_part
            grad_down[...] += down_part

    add_up(0)

    @pl.when(section == 0)
    def _():
        forward_back(batches - 1)

    loop(batches, add_up, 1)

    def sent(b):
        exchanged(out_a, in_a, send_a, recv_a, b).wait_send()
        exchanged(out_b, in_b, send_b, recv_b, b).wait_send()
        exchanged(out_r, in_r, send_r, recv_r, b).wait_send()
        carry(b).wait_send()

    loop(batches, sent)
    left(all_rows, 0)
    left(all_scaled, 1)
    left(all_act, 2)
    left(all_back, 3)


def shards(tokens, routes, gate_probs, w_gate, w_up, w_down, cotangent):
    micro_count, row_count, width = tokens.shape
    top = routes.shape[-1]
    experts = lax.axis_size("expert")
    n_dp = lax.axis_size("dp")
    cap = min(row_count, row_count * top // experts + 1)
    hidden = w_gate.shape[-1]
    batches, tokens_b = micro_count, row_count
    slots = experts * cap
    pieces = width // LANES
    part = width // n_dp

    def in_hbm(array):
        return pltpu.with_memory_space_constraint(array, pltpu.HBM)

    any_ = pl.BlockSpec(memory_space=pl.ANY)
    vmem = pl.BlockSpec(memory_space=pltpu.VMEM)
    dma = pltpu.SemaphoreType.DMA
    outs = pl.pallas_call(
        functools.partial(kernel, (batches, tokens_b, slots, cap, top, experts, n_dp)),
        out_shape=[
            jax.ShapeDtypeStruct((part, hidden), F32),
            jax.ShapeDtypeStruct((part, hidden), F32),
            jax.ShapeDtypeStruct((hidden, part), F32),
        ],
        in_specs=[any_] * 7,
        out_specs=[vmem] * 3,
        scratch_shapes=[
            pltpu.VMEM((batches, top, tokens_b), jnp.int32),
            pltpu.VMEM((batches, top, tokens_b), F32),
            pltpu.VMEM((width, 2 * hidden), BF16),
            pltpu.VMEM((hidden, width), BF16),
            pltpu.VMEM((2 * hidden, width), BF16),
            pltpu.VMEM((width, hidden), BF16),
            pltpu.VMEM((batches, tokens_b, width), BF16),
            pltpu.VMEM((batches, slots, tokens_b * top), BF16),
            pltpu.VMEM((batches, tokens_b * top, slots), BF16),
            pltpu.VMEM((batches, tokens_b * top, 1), F32),
            *[pltpu.VMEM((batches, slots, pieces, LANES), BF16)] * 6,
            *[pltpu.VMEM((batches, tokens_b, width), BF16)] * 2,
            *[pltpu.VMEM((batches, slots, width), BF16)] * 2,
            pltpu.VMEM((slots, width), BF16),
            pltpu.VMEM((batches, slots, 2 * hidden), F32),
            *[pltpu.VMEM((batches, n_dp, slots, part), BF16)] * 2,
            pltpu.VMEM((batches, n_dp, slots, 2 * hidden), BF16),
            pltpu.VMEM((batches, n_dp, slots, hidden), BF16),
            pltpu.VMEM((slots * pieces, LANES), F32),
            dma((6,)),
            *[dma((batches,))] * 6,
            *[dma((batches,))] * 2,
            dma((4,)),
            dma((4, n_dp, batches)),
        ],
        compiler_params=pltpu.CompilerParams(
            collective_id=0, has_side_effects=True, vmem_limit_bytes=46 * 1024 * 1024
        ),
    )(
        in_hbm(tokens), in_hbm(cotangent),
        in_hbm(routes[0].transpose(0, 2, 1)), in_hbm(gate_probs[0].transpose(0, 2, 1)),
        in_hbm(w_gate[0, 0]), in_hbm(w_up[0, 0]), in_hbm(w_down[0, 0]),
    )
    return tuple(out[None, None] for out in outs)


def solution(mesh):
    in_specs = (
        P(None, ("expert", "dp"), None),
        P("section", None, ("expert", "dp"), None),
        P("section", None, ("expert", "dp"), None),
        P("section", "expert", None, None),
        P("section", "expert", None, None),
        P("section", "expert", None, None),
        P(None, ("expert", "dp"), None),
    )
    out_specs = (
        P("section", "expert", "dp", None),
        P("section", "expert", "dp", None),
        P("section", "expert", None, "dp"),
    )
    return jax.shard_map(shards, mesh=mesh, in_specs=in_specs, out_specs=out_specs, check_vma=False)
```

```python
import functools
import jax
import jax.numpy as jnp
from jax import lax
from jax.experimental import pallas as pl
from jax.experimental.pallas import tpu as pltpu
from jax.sharding import PartitionSpec as P

F32, BF16 = jnp.float32, jnp.bfloat16
epsilon = 1e-05
MESH = pl.DeviceIdType.MESH
LANES = 128
rows_by_rows = (((0,), (0,)), ((), ()))
cols_by_cols = (((1,), (1,)), ((), ()))


def inverse_rms(values):
    return lax.rsqrt(jnp.mean(values * values, -1, keepdims=True) + epsilon)


def matmul(a, b, dims=(((1,), (0,)), ((), ()))):
    return lax.dot_general(a, b, dims, preferred_element_type=F32)


def kernel(
    sizes,
    tokens, cotangent, ids_hbm, probs_hbm, gate_hbm, up_hbm, down_hbm,
    grad_gate, grad_up, grad_down,
    ids, probs, w_hidden, w_down, w_hidden_t, w_down_t, base, select, select_t, weights,
    out_a, out_b, out_r, in_a, in_b, in_r,
    carry_out, carry_in, rows, scaled_rows, work, pre_hidden,
    all_rows, all_scaled, all_back, all_act, spread,
    early_out, early_in, ids_in, probs_in, tiles_out, tiles_in,
    load_sem, send_a, send_b, send_r, recv_a, recv_b, recv_r,
    send_carry, recv_carry, send_dp, recv_dp,
    send_early, recv_early,
):
    batches, tokens_b, slots, cap, top, experts, n_dp = sizes
    width = base.shape[-1]
    units = w_down.shape[0]
    pieces = width // LANES
    part = width // n_dp
    pairs = tokens_b * top
    section = lax.axis_index("section")
    me = lax.axis_index("expert")
    z = lax.axis_index("dp")

    def expert_at(p):
        return lax.rem(me + p, experts)

    def dp_at(q):
        return lax.rem(z + q, n_dp)

    loads = [
        pltpu.make_async_copy(gate_hbm, w_hidden.at[:, pl.ds(0, units)], load_sem.at[0]),
        pltpu.make_async_copy(up_hbm, w_hidden.at[:, pl.ds(units, units)], load_sem.at[1]),
        pltpu.make_async_copy(down_hbm, w_down, load_sem.at[2]),
    ]

    @pl.when(section == 0)
    def _():
        pltpu.make_async_copy(tokens, base, load_sem.at[3]).start()

    @pl.when(section == 1)
    def _():
        pltpu.make_async_copy(cotangent, base, load_sem.at[3]).start()

    tables = [
        pltpu.make_async_copy(ids_hbm, ids, load_sem.at[4]),
        pltpu.make_async_copy(probs_hbm, probs, load_sem.at[5]),
    ]
    for load in tables + loads:
        load.start()

    barrier = pltpu.get_barrier_semaphore()

    def greet(p, _):
        pl.semaphore_signal(barrier, inc=1, device_id={"expert": expert_at(p)}, device_id_type=MESH)
        return 0

    lax.fori_loop(1, experts, greet, 0)
    for q in range(1, n_dp):
        pl.semaphore_signal(barrier, inc=1, device_id={"dp": dp_at(q)}, device_id_type=MESH)
    pl.semaphore_signal(barrier, inc=1, device_id={"section": 1 - section}, device_id_type=MESH)

    def upright(row):
        size = row.shape[-1]
        along = lax.broadcasted_iota(jnp.int32, (size, size), 1)
        down = lax.broadcasted_iota(jnp.int32, (size, size), 0)
        return jnp.sum(jnp.where(along == down, row, 0.0), 1, keepdims=True)

    def places(named_ids, by_slot=False):
        named_row = named_ids.astype(F32)
        own = jnp.concatenate([upright(named_row[k:k + 1]) for k in range(top)], 0).astype(jnp.int32)
        order_l = lax.broadcasted_iota(jnp.int32, (pairs, pairs), 1)
        order_s = lax.broadcasted_iota(jnp.int32, (pairs, pairs), 0)
        before = jnp.where(order_l < order_s, 1.0, 0.0).astype(BF16)
        one_hot = jnp.where(own == lax.broadcasted_iota(jnp.int32, (pairs, experts), 1), 1.0, 0.0)
        earlier = matmul(before, one_hot.astype(BF16))
        rank = jnp.sum(earlier * one_hot, 1, keepdims=True)
        relative = own - me
        relative = jnp.where(relative < 0, relative + experts, relative)
        relative = relative.astype(F32)
        target = rank * experts + relative if by_slot else relative * cap + rank
        target_row = jnp.sum(jnp.where(order_l == order_s, target, 0.0), 0, keepdims=True)
        return target, target_row

    def selector(target_row):
        lines = lax.broadcasted_iota(jnp.int32, (slots, pairs), 0).astype(F32)
        return jnp.where(lines == target_row, 1.0, 0.0).astype(BF16)

    def weights_of(prob_row):
        return jnp.concatenate([upright(prob_row[k:k + 1]) for k in range(top)], 0)

    def selectors(b):
        weights[b] = weights_of(probs[b])
        target, target_row = places(ids[b])
        columns = lax.broadcasted_iota(jnp.int32, (pairs, slots), 1).astype(F32)
        select_t[b] = jnp.where(columns == target, 1.0, 0.0).astype(BF16)
        select[b] = selector(target_row)

    for load in tables:
        load.wait()
    pltpu.make_async_copy(tokens, base, load_sem.at[3]).wait()

    def pack(values, out, own, b):
        for j in range(pieces):
            spread[pl.ds(j, slots, stride=pieces), :] = values[:, j * LANES:(j + 1) * LANES]
        out[b] = spread[...].reshape(slots, pieces, LANES).astype(BF16)
        own[b, 0:cap] = out[b, 0:cap]

    def unpack(tiles, ref):
        spread[...] = tiles.astype(F32).reshape(slots * pieces, LANES)
        for j in range(pieces):
            ref[:, j * LANES:(j + 1) * LANES] = spread[pl.ds(j, slots, stride=pieces), :].astype(BF16)

    chunk = cap

    def exchange(out, into, send_sem, recv_sem, b, sign):
        def one(p, _):
            place = pl.ds(p * chunk, chunk)
            to = lax.rem(me + sign * p + experts, experts)
            pltpu.make_async_remote_copy(
                src_ref=out.at[b, place], dst_ref=into.at[b, place],
                send_sem=send_sem.at[b], recv_sem=recv_sem.at[b],
                device_id={"expert": to}, device_id_type=MESH,
            ).start()
            return 0

        lax.fori_loop(1, experts, one, 0)

    def exchanged(out, into, send_sem, recv_sem, b):
        others = pl.ds(chunk, slots - chunk)
        return pltpu.make_async_remote_copy(
            src_ref=out.at[b, others], dst_ref=into.at[b, others],
            send_sem=send_sem.at[b], recv_sem=recv_sem.at[b],
            device_id={"expert": expert_at(1)}, device_id_type=MESH,
        )

    def carry(b):
        return pltpu.make_async_remote_copy(
            src_ref=carry_out.at[b], dst_ref=carry_in.at[b],
            send_sem=send_carry.at[b], recv_sem=recv_carry.at[b],
            device_id={"section": 1 - section}, device_id_type=MESH,
        )

    def to_dp(src, into, which, b, q, to):
        return pltpu.make_async_remote_copy(
            src_ref=src, dst_ref=into.at[b, q],
            send_sem=send_dp.at[which], recv_sem=recv_dp.at[which, q, b],
            device_id={"dp": to}, device_id_type=MESH,
        )

    def share_part(source, into, which, b):
        for q in range(1, n_dp):
            lanes = pl.ds(pl.multiple_of(dp_at(q) * part, part), part)
            to_dp(source.at[b, :, lanes], into, which, b, q, dp_at(q)).start()

    def share(into, which, b):
        for q in (1, n_dp - 1):
            to_dp(into.at[b, 0], into, which, b, q, dp_at(q)).start()

    def arrived(into, which, b, q):
        to_dp(into.at[b, q], into, which, b, q, dp_at(1)).wait_recv()

    def forward(into, which, b, q):
        arrived(into, which, b, q)
        to_dp(into.at[b, q], into, which, b, 2, dp_at(q)).start()

    def left(into, which):
        others = into.at[:, pl.ds(1, n_dp - 1)]
        pltpu.make_async_remote_copy(
            src_ref=others, dst_ref=others,
            send_sem=send_dp.at[which], recv_sem=recv_dp.at[which, 0, 0],
            device_id={"dp": dp_at(1)}, device_id_type=MESH,
        ).wait_send()

    pieces_part = part // LANES
    cap_all = cap * batches

    def early(src, dst, which, q, to):
        return pltpu.make_async_remote_copy(
            src_ref=src, dst_ref=dst, send_sem=send_early.at[which], recv_sem=recv_early.at[which, q],
            device_id={"dp": to}, device_id_type=MESH,
        )

    def early_tiles(q, p, sem, to):
        return pltpu.make_async_remote_copy(
            src_ref=tiles_out.at[q, p], dst_ref=tiles_in.at[q, p],
            send_sem=send_early.at[3], recv_sem=recv_early.at[3, sem],
            device_id={"expert": to}, device_id_type=MESH,
        )

    def early_send(source, b):
        for q in range(1, n_dp):
            lanes = pl.ds(pl.multiple_of(dp_at(q) * part, part), part)
            early(source.at[b, :, lanes], early_in.at[q, b], 0, q, dp_at(q)).start()

    def early_tables():
        for q in range(1, n_dp):
            early(ids, ids_in.at[q], 1, q, dp_at(q)).start()
            early(probs, probs_in.at[q], 2, q, dp_at(q)).start()

    def early_dispatch(q):
        for which, into in enumerate((early_in, ids_in, probs_in)):
            early(into.at[q], into.at[q], which, q, dp_at(1)).wait_recv()
        for b in range(batches):
            picked = selector(places(ids_in[q, b], True)[1])
            weight = weights_of(probs_in[q, b])
            values = early_in[q, b].astype(F32)
            scaled = jnp.concatenate(
                [
                    (jnp.where(section == 0, 1.0, weight[k * tokens_b:(k + 1) * tokens_b]) * values).astype(BF16)
                    for k in range(top)
                ],
                0,
            )
            out = matmul(picked, scaled)
            for slot in range(cap):
                for j in range(pieces_part):
                    spread[pl.ds(j * cap_all + b * cap + slot, experts, stride=cap_all * pieces_part), :] = out[
                        slot * experts:(slot + 1) * experts, j * LANES:(j + 1) * LANES
                    ]
        tiles_out[q] = spread[...].reshape(experts, cap_all * pieces_part, LANES).astype(BF16)
        tiles_in[q, 0] = tiles_out[q, 0]

        def one(p, _):
            early_tiles(q, p, q, expert_at(p)).start()
            return 0

        lax.fori_loop(1, experts, one, 0)

    def early_take(q):
        early_tiles(q, pl.ds(1, experts - 1), q, expert_at(1)).wait_recv()
        spread[...] = tiles_in[q].astype(F32).reshape(slots * pieces, LANES)
        down = lax.broadcasted_iota(jnp.int32, (slots, slots), 0)
        along = lax.broadcasted_iota(jnp.int32, (slots, slots), 1)
        order = jnp.where(lax.rem(down, cap) * experts + down // cap == along, 1.0, 0.0).astype(BF16)
        for b in range(batches):
            for slot in range(cap):
                for j in range(pieces_part):
                    work[slot * experts:(slot + 1) * experts, j * LANES:(j + 1) * LANES] = spread[
                        pl.ds(j * cap_all + b * cap + slot, experts, stride=cap_all * pieces_part), :
                    ].astype(BF16)
            block = matmul(order, work[:, 0:part]).astype(BF16)

            @pl.when(section == 0)
            def _():
                all_rows[b, q] = block

            @pl.when(section == 1)
            def _():
                all_scaled[b, q] = block

    mine = pl.ds(pl.multiple_of(z * part, part), part)

    def pack_rows(b, current):
        normed = (current * inverse_rms(current)).astype(BF16)
        chosen = select[b, :, 0:tokens_b] + select[b, :, tokens_b:pairs]
        pack(matmul(chosen, normed), out_a, in_a, b)
        early_out[b] = normed

    def dispatch_rows(b, current):
        pack_rows(b, current)
        send_rows(b)

    def send_rows(b):
        exchange(out_a, in_a, send_a, recv_a, b, 1)

    def pack_scaled(b, upstream):
        scaled = jnp.concatenate(
            [(weights[b, k * tokens_b:(k + 1) * tokens_b] * upstream).astype(BF16) for k in range(top)], 0
        )
        pack(matmul(select[b], scaled), out_b, in_b, b)

    def dispatch_scaled(b, upstream):
        pack_scaled(b, upstream)
        send_scaled(b)

    def send_scaled(b):
        exchange(out_b, in_b, send_b, recv_b, b, 1)

    def take_rows(b):
        exchanged(out_a, in_a, send_a, recv_a, b).wait_recv()
        unpack(in_a[b], rows.at[b])
        all_rows[b, 0] = rows[b, :, mine]

        @pl.when(section == 1)
        def _():
            share_part(rows, all_rows, 0, b)

    def take_scaled(b):
        exchanged(out_b, in_b, send_b, recv_b, b).wait_recv()
        unpack(in_b[b], scaled_rows.at[b])
        all_scaled[b, 0] = scaled_rows[b, :, mine]

        @pl.when(section == 0)
        def _():
            share_part(scaled_rows, all_scaled, 1, b)

    def hidden(b):
        pre = matmul(rows[b], w_hidden[...])
        pre_hidden[b] = pre
        g, u = pre[:, 0:units], pre[:, units:2 * units]
        all_act[b, 0] = (g * jax.nn.sigmoid(g) * u).astype(BF16)
        share(all_act, 2, b)

    def produce(b):
        pack(matmul(all_act[b, 0], w_down[...]), out_r, in_r, b)
        exchange(out_r, in_r, send_r, recv_r, b, -1)

    def hidden_back(b):
        back = matmul(scaled_rows[b], w_down_t[...])
        g, u = pre_hidden[b, :, 0:units], pre_hidden[b, :, units:2 * units]
        sg = jax.nn.sigmoid(g)
        all_back[b, 0, :, 0:units] = (back * u * sg * (1.0 + g * (1.0 - sg))).astype(BF16)
        all_back[b, 0, :, units:2 * units] = (back * (g * sg)).astype(BF16)
        share(all_back, 3, b)

    def produce_back(b):
        pack(matmul(all_back[b, 0], w_hidden_t[...]), out_r, in_r, b)
        exchange(out_r, in_r, send_r, recv_r, b, -1)

    def turn_down(b):
        place = pl.ds(pl.multiple_of(b * (width // batches), width // batches), width // batches)
        w_down_t[place, :] = w_down[:, place].T

    def turn_hidden(b):
        place = pl.ds(pl.multiple_of(b * (width // batches), width // batches), width // batches)
        w_hidden_t[:, place] = w_hidden[place, :].T

    def take_returned(b):
        exchanged(out_r, in_r, send_r, recv_r, b).wait_recv()
        unpack(in_r[b], work)
        return matmul(select_t[b], work[...])

    def combine(b):
        chosen = take_returned(b)
        total = weights[b, 0:tokens_b] * chosen[0:tokens_b]
        for k in range(1, top):
            part_k = slice(k * tokens_b, (k + 1) * tokens_b)
            total = total + weights[b, part_k] * chosen[part_k]
        carry_out[b] = (base[b].astype(F32) + total).astype(BF16)
        carry(b).start()

    def combine_back(b):
        chosen = take_returned(b)
        d_normed = chosen[0:tokens_b]
        for k in range(1, top):
            d_normed = d_normed + chosen[k * tokens_b:(k + 1) * tokens_b]
        current = carry_in[b].astype(F32)
        scale = inverse_rms(current)
        back = scale * d_normed - current * (scale * scale * scale) * jnp.mean(
            d_normed * current, -1, keepdims=True
        )
        carry_out[b] = (base[b].astype(F32) + back).astype(BF16)
        carry(b).start()

    def forward_act(b):
        @pl.when(lax.rem(b, 2) == 0)
        def _():
            forward(all_act, 2, b, 1)

        @pl.when(lax.rem(b, 2) == 1)
        def _():
            forward(all_act, 2, b, n_dp - 1)

    def forward_back(b):
        for q, lanes in ((1, pl.ds(0, units)), (n_dp - 1, pl.ds(units, units))):
            arrived(all_back, 3, b, q)
            pltpu.make_async_remote_copy(
                src_ref=all_back.at[b, q, :, lanes], dst_ref=all_back.at[b, 2, :, lanes],
                send_sem=send_dp.at[3], recv_sem=recv_dp.at[3, 2, b],
                device_id={"dp": dp_at(q)}, device_id_type=MESH,
            ).start()

    def all_arrived(b):
        @pl.when(section == 0)
        def _():
            for q in range(1, n_dp):
                arrived(all_scaled, 1, b, q)

        @pl.when(section == 1)
        def _():
            for q in range(1, n_dp):
                arrived(all_rows, 0, b, q)

        @pl.when(lax.rem(b, 2) == 0)
        def _():
            arrived(all_act, 2, b, n_dp - 1)

        @pl.when(lax.rem(b, 2) == 1)
        def _():
            arrived(all_act, 2, b, 1)

        arrived(all_act, 2, b, 2)
        arrived(all_back, 3, b, 2)

    def wait_loads():
        for load in loads:
            load.wait()

    def loop(count, body, first=0):
        def step(i, _):
            body(i)
            return 0

        lax.fori_loop(first, count, step, 0)

    selectors(0)

    @pl.when(section == 0)
    def _():
        pack_rows(0, base[0].astype(F32))

    @pl.when(section == 1)
    def _():
        pack_scaled(0, base[0].astype(F32))

    pl.semaphore_wait(barrier, experts - 1 + n_dp - 1 + 1)

    @pl.when(section == 0)
    def _():
        def start(b):
            selectors(b)
            dispatch_rows(b, base[b].astype(F32))
            early_send(early_out, b)

        send_rows(0)
        early_send(early_out, 0)
        early_tables()
        loop(batches, start, 1)
        wait_loads()

        def forward_step(i):
            @pl.when(i < batches)
            def _():
                take_rows(i)
                hidden(i)
                produce(i)

            @pl.when(i >= 1)
            def _():
                combine(i - 1)

        loop(batches + 1, forward_step)
        loop(batches, turn_down)
        loop(n_dp, early_dispatch, 1)

        def backward(i):
            @pl.when(i < batches)
            def _():
                carry(i).wait_recv()
                dispatch_scaled(i, carry_in[i].astype(F32))
                forward_act(i)

            @pl.when(i >= 1)
            def _():
                take_scaled(i - 1)
                hidden_back(i - 1)

            @pl.when(i >= 2)
            def _():
                forward_back(i - 2)

        loop(batches + 1, backward)

    @pl.when(section == 1)
    def _():
        def start(b):
            selectors(b)
            dispatch_scaled(b, base[b].astype(F32))
            early_send(base, b)

        send_scaled(0)
        loop(batches, lambda b: early_send(base, b))
        early_tables()

        def start(b):
            selectors(b)
            pack_scaled(b, base[b].astype(F32))

        loop(batches, start, 1)
        loop(2, send_scaled, 1)
        wait_loads()
        loop(batches, turn_down)
        loop(batches, turn_hidden)

        def both(i):
            @pl.when(i < batches)
            def _():
                carry(i).wait_recv()
                dispatch_rows(i, carry_in[i].astype(F32))

            @pl.when(i + 2 < batches)
            def _():
                send_scaled(i + 2)

            @pl.when((i >= 1) & (i < batches + 1))
            def _():
                take_rows(i - 1)
                hidden(i - 1)
                take_scaled(i - 1)
                hidden_back(i - 1)
                produce_back(i - 1)

            @pl.when(i >= 2)
            def _():
                combine_back(i - 2)
                forward_act(i - 2)
                forward_back(i - 2)

        loop(batches + 2, both)
        loop(n_dp, early_dispatch, 1)

    def add_up(b):
        all_arrived(b)

        def flat(ref):
            return ref[b].reshape(n_dp * slots, ref.shape[-1])

        both = matmul(flat(all_rows), flat(all_back), rows_by_rows)
        gate_part, up_part = both[:, 0:units], both[:, units:2 * units]
        down_part = matmul(flat(all_act), flat(all_scaled), rows_by_rows)

        @pl.when(b == 0)
        def _():
            grad_gate[...] = gate_part
            grad_up[...] = up_part
            grad_down[...] = down_part

        @pl.when(b > 0)
        def _():
            grad_gate[...] += gate_part
            grad_up[...] += up_part
            grad_down[...] += down_part

    loop(n_dp, early_take, 1)
    add_up(0)

    @pl.when(section == 0)
    def _():
        forward_back(batches - 1)

    loop(batches, add_up, 1)

    def sent(b):
        exchanged(out_a, in_a, send_a, recv_a, b).wait_send()
        exchanged(out_b, in_b, send_b, recv_b, b).wait_send()
        exchanged(out_r, in_r, send_r, recv_r, b).wait_send()
        carry(b).wait_send()

    loop(batches, sent)
    @pl.when(section == 0)
    def _():
        left(all_scaled, 1)

    @pl.when(section == 1)
    def _():
        left(all_rows, 0)

    for which, into in enumerate((early_in, ids_in, probs_in)):
        early(into.at[pl.ds(1, n_dp - 1)], into.at[pl.ds(1, n_dp - 1)], which, 0, dp_at(1)).wait_send()
    early_tiles(pl.ds(1, n_dp - 1), pl.ds(1, experts - 1), 0, expert_at(1)).wait_send()
    left(all_act, 2)
    left(all_back, 3)


def hand_over(*refs):
    copies = [pltpu.make_async_copy(refs[i], refs[3 + i], refs[6].at[i]) for i in range(3)]
    for copy in copies:
        copy.start()
    for copy in copies:
        copy.wait()


def shards(tokens, routes, gate_probs, w_gate, w_up, w_down, cotangent):
    micro_count, row_count, width = tokens.shape
    top = routes.shape[-1]
    experts = lax.axis_size("expert")
    n_dp = lax.axis_size("dp")
    cap = min(row_count, row_count * top // experts + 1)
    hidden = w_gate.shape[-1]
    batches, tokens_b = micro_count, row_count
    slots = experts * cap
    pieces = width // LANES
    part = width // n_dp

    def in_hbm(array):
        return pltpu.with_memory_space_constraint(array, pltpu.HBM)

    any_ = pl.BlockSpec(memory_space=pl.ANY)
    vmem = pl.BlockSpec(memory_space=pltpu.VMEM)
    dma = pltpu.SemaphoreType.DMA
    outs = pl.pallas_call(
        functools.partial(kernel, (batches, tokens_b, slots, cap, top, experts, n_dp)),
        out_shape=[
            jax.ShapeDtypeStruct((part, hidden), F32),
            jax.ShapeDtypeStruct((part, hidden), F32),
            jax.ShapeDtypeStruct((hidden, part), F32),
        ],
        in_specs=[any_] * 7,
        out_specs=[vmem] * 3,
        scratch_shapes=[
            pltpu.VMEM((batches, top, tokens_b), jnp.int32),
            pltpu.VMEM((batches, top, tokens_b), F32),
            pltpu.VMEM((width, 2 * hidden), BF16),
            pltpu.VMEM((hidden, width), BF16),
            pltpu.VMEM((2 * hidden, width), BF16),
            pltpu.VMEM((width, hidden), BF16),
            pltpu.VMEM((batches, tokens_b, width), BF16),
            pltpu.VMEM((batches, slots, tokens_b * top), BF16),
            pltpu.VMEM((batches, tokens_b * top, slots), BF16),
            pltpu.VMEM((batches, tokens_b * top, 1), F32),
            *[pltpu.VMEM((batches, slots, pieces, LANES), BF16)] * 6,
            *[pltpu.VMEM((batches, tokens_b, width), BF16)] * 2,
            *[pltpu.VMEM((batches, slots, width), BF16)] * 2,
            pltpu.VMEM((slots, width), BF16),
            pltpu.VMEM((batches, slots, 2 * hidden), F32),
            *[pltpu.VMEM((batches, n_dp, slots, part), BF16)] * 2,
            pltpu.VMEM((batches, n_dp, slots, 2 * hidden), BF16),
            pltpu.VMEM((batches, n_dp, slots, hidden), BF16),
            pltpu.VMEM((slots * pieces, LANES), F32),
            pltpu.VMEM((batches, tokens_b, width), BF16),
            pltpu.VMEM((n_dp, batches, tokens_b, part), BF16),
            pltpu.VMEM((n_dp, batches, top, tokens_b), jnp.int32),
            pltpu.VMEM((n_dp, batches, top, tokens_b), F32),
            *[pltpu.VMEM((n_dp, experts, cap * batches * part // LANES, LANES), BF16)] * 2,
            dma((6,)),
            *[dma((batches,))] * 6,
            *[dma((batches,))] * 2,
            dma((4,)),
            dma((4, n_dp, batches)),
            dma((4,)),
            dma((4, n_dp)),
        ],
        compiler_params=pltpu.CompilerParams(
            collective_id=0, has_side_effects=True, vmem_limit_bytes=50 * 1024 * 1024
        ),
    )(
        in_hbm(tokens), in_hbm(cotangent),
        in_hbm(routes[0].transpose(0, 2, 1)), in_hbm(gate_probs[0].transpose(0, 2, 1)),
        in_hbm(w_gate[0, 0]), in_hbm(w_up[0, 0]), in_hbm(w_down[0, 0]),
    )
    outs = pl.pallas_call(
        hand_over,
        out_shape=[pltpu.HBM(out.shape, out.dtype) for out in outs],
        in_specs=[any_] * 3,
        out_specs=[any_] * 3,
        scratch_shapes=[dma((3,))],
        compiler_params=pltpu.CompilerParams(vmem_limit_bytes=4 * 1024 * 1024),
    )(*outs)
    return tuple(out[None, None] for out in outs)


def solution(mesh):
    in_specs = (
        P(None, ("expert", "dp"), None),
        P("section", None, ("expert", "dp"), None),
        P("section", None, ("expert", "dp"), None),
        P("section", "expert", None, None),
        P("section", "expert", None, None),
        P("section", "expert", None, None),
        P(None, ("expert", "dp"), None),
    )
    out_specs = (
        P("section", "expert", "dp", None),
        P("section", "expert", "dp", None),
        P("section", "expert", None, "dp"),
    )
    return jax.shard_map(shards, mesh=mesh, in_specs=in_specs, out_specs=out_specs, check_vma=False)
```

```python
import functools
import jax
import jax.numpy as jnp
from jax import lax
from jax.experimental import pallas as pl
from jax.experimental.pallas import tpu as pltpu
from jax.sharding import PartitionSpec as P

F32, BF16 = jnp.float32, jnp.bfloat16
epsilon = 1e-05
MESH = pl.DeviceIdType.MESH
LANES = 128
rows_by_rows = (((0,), (0,)), ((), ()))
cols_by_cols = (((1,), (1,)), ((), ()))


def inverse_rms(values):
    return lax.rsqrt(jnp.mean(values * values, -1, keepdims=True) + epsilon)


def matmul(a, b, dims=(((1,), (0,)), ((), ()))):
    return lax.dot_general(a, b, dims, preferred_element_type=F32)


def kernel(
    sizes,
    tokens, cotangent, ids_hbm, probs_hbm, gate_hbm, up_hbm, down_hbm,
    grad_gate, grad_up, grad_down,
    ids, probs, w_hidden, w_down, w_hidden_t, w_down_t, base, select, select_t, weights,
    out_a, out_b, out_r, in_a, in_b, in_r,
    carry_out, carry_in, rows, scaled_rows, work, pre_hidden,
    all_rows, all_scaled, all_back, all_act, spread,
    early_out, early_in, ids_in, probs_in, tiles_out, tiles_in,
    load_sem, send_a, send_b, send_r, recv_a, recv_b, recv_r,
    send_carry, recv_carry, send_dp, recv_dp,
    send_early, recv_early,
):
    batches, tokens_b, slots, cap, top, experts, n_dp = sizes
    width = base.shape[-1]
    units = w_down.shape[0]
    pieces = width // LANES
    part = width // n_dp
    pairs = tokens_b * top
    section = lax.axis_index("section")
    me = lax.axis_index("expert")
    z = lax.axis_index("dp")

    def expert_at(p):
        return lax.rem(me + p, experts)

    def dp_at(q):
        return lax.rem(z + q, n_dp)

    loads = [
        pltpu.make_async_copy(gate_hbm, w_hidden.at[:, pl.ds(0, units)], load_sem.at[0]),
        pltpu.make_async_copy(up_hbm, w_hidden.at[:, pl.ds(units, units)], load_sem.at[1]),
        pltpu.make_async_copy(down_hbm, w_down, load_sem.at[2]),
    ]

    @pl.when(section == 0)
    def _():
        pltpu.make_async_copy(tokens, base, load_sem.at[3]).start()

    @pl.when(section == 1)
    def _():
        pltpu.make_async_copy(cotangent, base, load_sem.at[3]).start()

    tables = [
        pltpu.make_async_copy(ids_hbm, ids, load_sem.at[4]),
        pltpu.make_async_copy(probs_hbm, probs, load_sem.at[5]),
    ]
    for load in tables + loads:
        load.start()

    barrier = pltpu.get_barrier_semaphore()

    def greet(p, _):
        pl.semaphore_signal(barrier, inc=1, device_id={"expert": expert_at(p)}, device_id_type=MESH)
        return 0

    lax.fori_loop(1, experts, greet, 0)
    for q in range(1, n_dp):
        pl.semaphore_signal(barrier, inc=1, device_id={"dp": dp_at(q)}, device_id_type=MESH)
    pl.semaphore_signal(barrier, inc=1, device_id={"section": 1 - section}, device_id_type=MESH)

    def upright(row):
        size = row.shape[-1]
        along = lax.broadcasted_iota(jnp.int32, (size, size), 1)
        down = lax.broadcasted_iota(jnp.int32, (size, size), 0)
        return jnp.sum(jnp.where(along == down, row, 0.0), 1, keepdims=True)

    def places(named_ids, by_slot=False):
        named_row = named_ids.astype(F32)
        own = jnp.concatenate([upright(named_row[k:k + 1]) for k in range(top)], 0).astype(jnp.int32)
        order_l = lax.broadcasted_iota(jnp.int32, (pairs, pairs), 1)
        order_s = lax.broadcasted_iota(jnp.int32, (pairs, pairs), 0)
        before = jnp.where(order_l < order_s, 1.0, 0.0).astype(BF16)
        one_hot = jnp.where(own == lax.broadcasted_iota(jnp.int32, (pairs, experts), 1), 1.0, 0.0)
        earlier = matmul(before, one_hot.astype(BF16))
        rank = jnp.sum(earlier * one_hot, 1, keepdims=True)
        relative = own - me
        relative = jnp.where(relative < 0, relative + experts, relative)
        relative = relative.astype(F32)
        target = rank * experts + relative if by_slot else relative * cap + rank
        target_row = jnp.sum(jnp.where(order_l == order_s, target, 0.0), 0, keepdims=True)
        return target, target_row

    def selector(target_row):
        lines = lax.broadcasted_iota(jnp.int32, (slots, pairs), 0).astype(F32)
        return jnp.where(lines == target_row, 1.0, 0.0).astype(BF16)

    def weights_of(prob_row):
        return jnp.concatenate([upright(prob_row[k:k + 1]) for k in range(top)], 0)

    def selectors(b):
        weights[b] = weights_of(probs[b])
        target, target_row = places(ids[b])
        columns = lax.broadcasted_iota(jnp.int32, (pairs, slots), 1).astype(F32)
        select_t[b] = jnp.where(columns == target, 1.0, 0.0).astype(BF16)
        select[b] = selector(target_row)

    for load in tables:
        load.wait()
    pltpu.make_async_copy(tokens, base, load_sem.at[3]).wait()

    def pack(values, out, own, b):
        for j in range(pieces):
            spread[pl.ds(j, slots, stride=pieces), :] = values[:, j * LANES:(j + 1) * LANES]
        out[b] = spread[...].reshape(slots, pieces, LANES).astype(BF16)
        own[b, 0:cap] = out[b, 0:cap]

    def unpack(tiles, ref):
        spread[...] = tiles.astype(F32).reshape(slots * pieces, LANES)
        for j in range(pieces):
            ref[:, j * LANES:(j + 1) * LANES] = spread[pl.ds(j, slots, stride=pieces), :].astype(BF16)

    chunk = cap

    def exchange(out, into, send_sem, recv_sem, b, sign):
        def one(p, _):
            place = pl.ds(p * chunk, chunk)
            to = lax.rem(me + sign * p + experts, experts)
            pltpu.make_async_remote_copy(
                src_ref=out.at[b, place], dst_ref=into.at[b, place],
                send_sem=send_sem.at[b], recv_sem=recv_sem.at[b],
                device_id={"expert": to}, device_id_type=MESH,
            ).start()
            return 0

        lax.fori_loop(1, experts, one, 0)

    def exchanged(out, into, send_sem, recv_sem, b):
        others = pl.ds(chunk, slots - chunk)
        return pltpu.make_async_remote_copy(
            src_ref=out.at[b, others], dst_ref=into.at[b, others],
            send_sem=send_sem.at[b], recv_sem=recv_sem.at[b],
            device_id={"expert": expert_at(1)}, device_id_type=MESH,
        )

    def carry(b):
        return pltpu.make_async_remote_copy(
            src_ref=carry_out.at[b], dst_ref=carry_in.at[b],
            send_sem=send_carry.at[b], recv_sem=recv_carry.at[b],
            device_id={"section": 1 - section}, device_id_type=MESH,
        )

    def to_dp(src, into, which, b, q, to):
        return pltpu.make_async_remote_copy(
            src_ref=src, dst_ref=into.at[b, q],
            send_sem=send_dp.at[which], recv_sem=recv_dp.at[which, q, b],
            device_id={"dp": to}, device_id_type=MESH,
        )

    def share_part(source, into, which, b):
        for q in range(1, n_dp):
            lanes = pl.ds(pl.multiple_of(dp_at(q) * part, part), part)
            to_dp(source.at[b, :, lanes], into, which, b, q, dp_at(q)).start()

    def share(into, which, b):
        for q in (1, n_dp - 1):
            to_dp(into.at[b, 0], into, which, b, q, dp_at(q)).start()

    def arrived(into, which, b, q):
        to_dp(into.at[b, q], into, which, b, q, dp_at(1)).wait_recv()

    def forward(into, which, b, q):
        arrived(into, which, b, q)
        to_dp(into.at[b, q], into, which, b, 2, dp_at(q)).start()

    def left(into, which):
        others = into.at[:, pl.ds(1, n_dp - 1)]
        pltpu.make_async_remote_copy(
            src_ref=others, dst_ref=others,
            send_sem=send_dp.at[which], recv_sem=recv_dp.at[which, 0, 0],
            device_id={"dp": dp_at(1)}, device_id_type=MESH,
        ).wait_send()

    pieces_part = part // LANES
    cap_all = cap * batches

    def early(src, dst, which, q, to):
        return pltpu.make_async_remote_copy(
            src_ref=src, dst_ref=dst, send_sem=send_early.at[which], recv_sem=recv_early.at[which, q],
            device_id={"dp": to}, device_id_type=MESH,
        )

    def early_tiles(q, p, sem, to):
        return pltpu.make_async_remote_copy(
            src_ref=tiles_out.at[q, p], dst_ref=tiles_in.at[q, p],
            send_sem=send_early.at[3], recv_sem=recv_early.at[3, sem],
            device_id={"expert": to}, device_id_type=MESH,
        )

    def early_send(source, b):
        for q in range(1, n_dp):
            lanes = pl.ds(pl.multiple_of(dp_at(q) * part, part), part)
            early(source.at[b, :, lanes], early_in.at[q, b], 0, q, dp_at(q)).start()

    def early_tables():
        for q in range(1, n_dp):
            early(ids, ids_in.at[q], 1, q, dp_at(q)).start()
            early(probs, probs_in.at[q], 2, q, dp_at(q)).start()

    def early_dispatch(q):
        for which, into in enumerate((early_in, ids_in, probs_in)):
            early(into.at[q], into.at[q], which, q, dp_at(1)).wait_recv()
        for b in range(batches):
            picked = selector(places(ids_in[q, b], True)[1])
            weight = weights_of(probs_in[q, b])
            values = early_in[q, b].astype(F32)
            scaled = jnp.concatenate(
                [
                    (jnp.where(section == 0, 1.0, weight[k * tokens_b:(k + 1) * tokens_b]) * values).astype(BF16)
                    for k in range(top)
                ],
                0,
            )
            out = matmul(picked, scaled)
            for slot in range(cap):
                for j in range(pieces_part):
                    spread[pl.ds(j * cap_all + b * cap + slot, experts, stride=cap_all * pieces_part), :] = out[
                        slot * experts:(slot + 1) * experts, j * LANES:(j + 1) * LANES
                    ]
        tiles_out[q] = spread[...].reshape(experts, cap_all * pieces_part, LANES).astype(BF16)
        tiles_in[q, 0] = tiles_out[q, 0]

        def one(p, _):
            early_tiles(q, p, q, expert_at(p)).start()
            return 0

        lax.fori_loop(1, experts, one, 0)

    def early_take(q):
        early_tiles(q, pl.ds(1, experts - 1), q, expert_at(1)).wait_recv()
        spread[...] = tiles_in[q].astype(F32).reshape(slots * pieces, LANES)
        down = lax.broadcasted_iota(jnp.int32, (slots, slots), 0)
        along = lax.broadcasted_iota(jnp.int32, (slots, slots), 1)
        order = jnp.where(lax.rem(down, cap) * experts + down // cap == along, 1.0, 0.0).astype(BF16)
        for b in range(batches):
            for slot in range(cap):
                for j in range(pieces_part):
                    work[slot * experts:(slot + 1) * experts, j * LANES:(j + 1) * LANES] = spread[
                        pl.ds(j * cap_all + b * cap + slot, experts, stride=cap_all * pieces_part), :
                    ].astype(BF16)
            block = matmul(order, work[:, 0:part]).astype(BF16)

            @pl.when(section == 0)
            def _():
                all_rows[b, q] = block

            @pl.when(section == 1)
            def _():
                all_scaled[b, q] = block

    mine = pl.ds(pl.multiple_of(z * part, part), part)

    def pack_rows(b, current):
        normed = (current * inverse_rms(current)).astype(BF16)
        chosen = select[b, :, 0:tokens_b] + select[b, :, tokens_b:pairs]
        pack(matmul(chosen, normed), out_a, in_a, b)
        early_out[b] = normed

    def dispatch_rows(b, current):
        pack_rows(b, current)
        send_rows(b)

    def send_rows(b):
        exchange(out_a, in_a, send_a, recv_a, b, 1)

    def pack_scaled(b, upstream):
        scaled = jnp.concatenate(
            [(weights[b, k * tokens_b:(k + 1) * tokens_b] * upstream).astype(BF16) for k in range(top)], 0
        )
        pack(matmul(select[b], scaled), out_b, in_b, b)

    def dispatch_scaled(b, upstream):
        pack_scaled(b, upstream)
        send_scaled(b)

    def send_scaled(b):
        exchange(out_b, in_b, send_b, recv_b, b, 1)

    def take_rows(b):
        exchanged(out_a, in_a, send_a, recv_a, b).wait_recv()
        unpack(in_a[b], rows.at[b])
        all_rows[b, 0] = rows[b, :, mine]

        @pl.when(section == 1)
        def _():
            share_part(rows, all_rows, 0, b)

    def take_scaled(b):
        exchanged(out_b, in_b, send_b, recv_b, b).wait_recv()
        unpack(in_b[b], scaled_rows.at[b])
        all_scaled[b, 0] = scaled_rows[b, :, mine]

        @pl.when(section == 0)
        def _():
            share_part(scaled_rows, all_scaled, 1, b)

    def hidden(b):
        pre = matmul(rows[b], w_hidden[...])
        pre_hidden[b] = pre
        g, u = pre[:, 0:units], pre[:, units:2 * units]
        all_act[b, 0] = (g * jax.nn.sigmoid(g) * u).astype(BF16)
        share(all_act, 2, b)

    def produce(b):
        pack(matmul(all_act[b, 0], w_down[...]), out_r, in_r, b)
        exchange(out_r, in_r, send_r, recv_r, b, -1)

    def hidden_back(b):
        back = matmul(scaled_rows[b], w_down_t[...])
        g, u = pre_hidden[b, :, 0:units], pre_hidden[b, :, units:2 * units]
        sg = jax.nn.sigmoid(g)
        all_back[b, 0, :, 0:units] = (back * u * sg * (1.0 + g * (1.0 - sg))).astype(BF16)
        all_back[b, 0, :, units:2 * units] = (back * (g * sg)).astype(BF16)
        share(all_back, 3, b)

    def produce_back(b):
        pack(matmul(all_back[b, 0], w_hidden_t[...]), out_r, in_r, b)
        exchange(out_r, in_r, send_r, recv_r, b, -1)

    def turn_down(b):
        place = pl.ds(pl.multiple_of(b * (width // batches), width // batches), width // batches)
        w_down_t[place, :] = w_down[:, place].T

    def turn_hidden(b):
        place = pl.ds(pl.multiple_of(b * (width // batches), width // batches), width // batches)
        w_hidden_t[:, place] = w_hidden[place, :].T

    def take_returned(b):
        exchanged(out_r, in_r, send_r, recv_r, b).wait_recv()
        unpack(in_r[b], work)
        return matmul(select_t[b], work[...])

    def combine(b):
        chosen = take_returned(b)
        total = weights[b, 0:tokens_b] * chosen[0:tokens_b]
        for k in range(1, top):
            part_k = slice(k * tokens_b, (k + 1) * tokens_b)
            total = total + weights[b, part_k] * chosen[part_k]
        carry_out[b] = (base[b].astype(F32) + total).astype(BF16)
        carry(b).start()

    def combine_back(b):
        chosen = take_returned(b)
        d_normed = chosen[0:tokens_b]
        for k in range(1, top):
            d_normed = d_normed + chosen[k * tokens_b:(k + 1) * tokens_b]
        current = carry_in[b].astype(F32)
        scale = inverse_rms(current)
        back = scale * d_normed - current * (scale * scale * scale) * jnp.mean(
            d_normed * current, -1, keepdims=True
        )
        carry_out[b] = (base[b].astype(F32) + back).astype(BF16)
        carry(b).start()

    def forward_act(b):
        @pl.when(lax.rem(b, 2) == 0)
        def _():
            forward(all_act, 2, b, 1)

        @pl.when(lax.rem(b, 2) == 1)
        def _():
            forward(all_act, 2, b, n_dp - 1)

    def forward_back(b):
        for q, lanes in ((1, pl.ds(0, units)), (n_dp - 1, pl.ds(units, units))):
            arrived(all_back, 3, b, q)
            pltpu.make_async_remote_copy(
                src_ref=all_back.at[b, q, :, lanes], dst_ref=all_back.at[b, 2, :, lanes],
                send_sem=send_dp.at[3], recv_sem=recv_dp.at[3, 2, b],
                device_id={"dp": dp_at(q)}, device_id_type=MESH,
            ).start()

    def all_arrived(b):
        @pl.when(section == 0)
        def _():
            for q in range(1, n_dp):
                arrived(all_scaled, 1, b, q)

        @pl.when(section == 1)
        def _():
            for q in range(1, n_dp):
                arrived(all_rows, 0, b, q)

        @pl.when(lax.rem(b, 2) == 0)
        def _():
            arrived(all_act, 2, b, n_dp - 1)

        @pl.when(lax.rem(b, 2) == 1)
        def _():
            arrived(all_act, 2, b, 1)

        arrived(all_act, 2, b, 2)
        arrived(all_back, 3, b, 2)

    def wait_loads():
        for load in loads:
            load.wait()

    def loop(count, body, first=0):
        def step(i, _):
            body(i)
            return 0

        lax.fori_loop(first, count, step, 0)

    selectors(0)

    @pl.when(section == 0)
    def _():
        pack_rows(0, base[0].astype(F32))

    @pl.when(section == 1)
    def _():
        pack_scaled(0, base[0].astype(F32))

    pl.semaphore_wait(barrier, experts - 1 + n_dp - 1 + 1)

    @pl.when(section == 0)
    def _():
        def start(b):
            selectors(b)
            dispatch_rows(b, base[b].astype(F32))
            early_send(early_out, b)

        send_rows(0)
        early_send(early_out, 0)
        early_tables()
        loop(batches, start, 1)
        wait_loads()

        def forward_step(i):
            @pl.when(i < batches)
            def _():
                take_rows(i)
                hidden(i)
                produce(i)

            @pl.when(i >= 1)
            def _():
                combine(i - 1)

        loop(batches + 1, forward_step)
        loop(batches, turn_down)
        loop(n_dp, early_dispatch, 1)

        def backward(i):
            @pl.when(i < batches)
            def _():
                carry(i).wait_recv()
                dispatch_scaled(i, carry_in[i].astype(F32))
                forward_act(i)

            @pl.when(i >= 1)
            def _():
                take_scaled(i - 1)
                hidden_back(i - 1)

            @pl.when(i >= 2)
            def _():
                forward_back(i - 2)

            @pl.when((i >= 1) & (i < n_dp))
            def _():
                early_take(i)

        loop(batches + 1, backward)

    @pl.when(section == 1)
    def _():
        def start(b):
            selectors(b)
            dispatch_scaled(b, base[b].astype(F32))
            early_send(base, b)

        send_scaled(0)
        loop(batches, lambda b: early_send(base, b))
        early_tables()

        def start(b):
            selectors(b)
            pack_scaled(b, base[b].astype(F32))

        loop(batches, start, 1)
        loop(2, send_scaled, 1)
        wait_loads()
        loop(batches, turn_down)
        loop(batches, turn_hidden)

        def both(i):
            @pl.when(i < batches)
            def _():
                carry(i).wait_recv()
                dispatch_rows(i, carry_in[i].astype(F32))

            @pl.when(i + 2 < batches)
            def _():
                send_scaled(i + 2)

            @pl.when((i >= 1) & (i < batches + 1))
            def _():
                take_rows(i - 1)
                hidden(i - 1)
                take_scaled(i - 1)
                hidden_back(i - 1)
                produce_back(i - 1)

            @pl.when(i >= 2)
            def _():
                combine_back(i - 2)
                forward_act(i - 2)
                forward_back(i - 2)

        loop(batches + 2, both)
        loop(n_dp, early_dispatch, 1)

    def add_up(b):
        all_arrived(b)

        def flat(ref):
            return ref[b].reshape(n_dp * slots, ref.shape[-1])

        both = matmul(flat(all_rows), flat(all_back), rows_by_rows)
        gate_part, up_part = both[:, 0:units], both[:, units:2 * units]
        down_part = matmul(flat(all_act), flat(all_scaled), rows_by_rows)

        @pl.when(b == 0)
        def _():
            grad_gate[...] = gate_part
            grad_up[...] = up_part
            grad_down[...] = down_part

        @pl.when(b > 0)
        def _():
            grad_gate[...] += gate_part
            grad_up[...] += up_part
            grad_down[...] += down_part

    @pl.when(section == 1)
    def _():
        loop(n_dp, early_take, 1)

    def finish(b):
        add_up(b)

        @pl.when((section == 0) & (b == 1))
        def _():
            forward_back(batches - 1)

    loop(batches, finish)

    def sent(b):
        exchanged(out_a, in_a, send_a, recv_a, b).wait_send()
        exchanged(out_b, in_b, send_b, recv_b, b).wait_send()
        exchanged(out_r, in_r, send_r, recv_r, b).wait_send()
        carry(b).wait_send()

    loop(batches, sent)
    @pl.when(section == 0)
    def _():
        left(all_scaled, 1)

    @pl.when(section == 1)
    def _():
        left(all_rows, 0)

    for which, into in enumerate((early_in, ids_in, probs_in)):
        early(into.at[pl.ds(1, n_dp - 1)], into.at[pl.ds(1, n_dp - 1)], which, 0, dp_at(1)).wait_send()
    early_tiles(pl.ds(1, n_dp - 1), pl.ds(1, experts - 1), 0, expert_at(1)).wait_send()
    left(all_act, 2)
    left(all_back, 3)


def hand_over(*refs):
    copies = [pltpu.make_async_copy(refs[i], refs[3 + i], refs[6].at[i]) for i in range(3)]
    for copy in copies:
        copy.start()
    for copy in copies:
        copy.wait()


def shards(tokens, routes, gate_probs, w_gate, w_up, w_down, cotangent):
    micro_count, row_count, width = tokens.shape
    top = routes.shape[-1]
    experts = lax.axis_size("expert")
    n_dp = lax.axis_size("dp")
    cap = min(row_count, row_count * top // experts + 1)
    hidden = w_gate.shape[-1]
    batches, tokens_b = micro_count, row_count
    slots = experts * cap
    pieces = width // LANES
    part = width // n_dp

    def in_hbm(array):
        return pltpu.with_memory_space_constraint(array, pltpu.HBM)

    any_ = pl.BlockSpec(memory_space=pl.ANY)
    vmem = pl.BlockSpec(memory_space=pltpu.VMEM)
    dma = pltpu.SemaphoreType.DMA
    outs = pl.pallas_call(
        functools.partial(kernel, (batches, tokens_b, slots, cap, top, experts, n_dp)),
        out_shape=[
            jax.ShapeDtypeStruct((part, hidden), F32),
            jax.ShapeDtypeStruct((part, hidden), F32),
            jax.ShapeDtypeStruct((hidden, part), F32),
        ],
        in_specs=[any_] * 7,
        out_specs=[vmem] * 3,
        scratch_shapes=[
            pltpu.VMEM((batches, top, tokens_b), jnp.int32),
            pltpu.VMEM((batches, top, tokens_b), F32),
            pltpu.VMEM((width, 2 * hidden), BF16),
            pltpu.VMEM((hidden, width), BF16),
            pltpu.VMEM((2 * hidden, width), BF16),
            pltpu.VMEM((width, hidden), BF16),
            pltpu.VMEM((batches, tokens_b, width), BF16),
            pltpu.VMEM((batches, slots, tokens_b * top), BF16),
            pltpu.VMEM((batches, tokens_b * top, slots), BF16),
            pltpu.VMEM((batches, tokens_b * top, 1), F32),
            *[pltpu.VMEM((batches, slots, pieces, LANES), BF16)] * 6,
            *[pltpu.VMEM((batches, tokens_b, width), BF16)] * 2,
            *[pltpu.VMEM((batches, slots, width), BF16)] * 2,
            pltpu.VMEM((slots, width), BF16),
            pltpu.VMEM((batches, slots, 2 * hidden), F32),
            *[pltpu.VMEM((batches, n_dp, slots, part), BF16)] * 2,
            pltpu.VMEM((batches, n_dp, slots, 2 * hidden), BF16),
            pltpu.VMEM((batches, n_dp, slots, hidden), BF16),
            pltpu.VMEM((slots * pieces, LANES), F32),
            pltpu.VMEM((batches, tokens_b, width), BF16),
            pltpu.VMEM((n_dp, batches, tokens_b, part), BF16),
            pltpu.VMEM((n_dp, batches, top, tokens_b), jnp.int32),
            pltpu.VMEM((n_dp, batches, top, tokens_b), F32),
            *[pltpu.VMEM((n_dp, experts, cap * batches * part // LANES, LANES), BF16)] * 2,
            dma((6,)),
            *[dma((batches,))] * 6,
            *[dma((batches,))] * 2,
            dma((4,)),
            dma((4, n_dp, batches)),
            dma((4,)),
            dma((4, n_dp)),
        ],
        compiler_params=pltpu.CompilerParams(
            collective_id=0, has_side_effects=True, vmem_limit_bytes=50 * 1024 * 1024
        ),
    )(
        in_hbm(tokens), in_hbm(cotangent),
        in_hbm(routes[0].transpose(0, 2, 1)), in_hbm(gate_probs[0].transpose(0, 2, 1)),
        in_hbm(w_gate[0, 0]), in_hbm(w_up[0, 0]), in_hbm(w_down[0, 0]),
    )
    outs = pl.pallas_call(
        hand_over,
        out_shape=[pltpu.HBM(out.shape, out.dtype) for out in outs],
        in_specs=[any_] * 3,
        out_specs=[any_] * 3,
        scratch_shapes=[dma((3,))],
        compiler_params=pltpu.CompilerParams(vmem_limit_bytes=4 * 1024 * 1024),
    )(*outs)
    return tuple(out[None, None] for out in outs)


def solution(mesh):
    in_specs = (
        P(None, ("expert", "dp"), None),
        P("section", None, ("expert", "dp"), None),
        P("section", None, ("expert", "dp"), None),
        P("section", "expert", None, None),
        P("section", "expert", None, None),
        P("section", "expert", None, None),
        P(None, ("expert", "dp"), None),
    )
    out_specs = (
        P("section", "expert", "dp", None),
        P("section", "expert", "dp", None),
        P("section", "expert", None, "dp"),
    )
    return jax.shard_map(shards, mesh=mesh, in_specs=in_specs, out_specs=out_specs, check_vma=False)
```

```python
import functools
import jax
import jax.numpy as jnp
from jax import lax
from jax.experimental import pallas as pl
from jax.experimental.pallas import tpu as pltpu
from jax.sharding import PartitionSpec as P

F32, BF16 = jnp.float32, jnp.bfloat16
epsilon = 1e-05
MESH = pl.DeviceIdType.MESH
LANES = 128
rows_by_rows = (((0,), (0,)), ((), ()))
cols_by_cols = (((1,), (1,)), ((), ()))


def inverse_rms(values):
    return lax.rsqrt(jnp.mean(values * values, -1, keepdims=True) + epsilon)


def matmul(a, b, dims=(((1,), (0,)), ((), ()))):
    return lax.dot_general(a, b, dims, preferred_element_type=F32)


def kernel(
    sizes,
    tokens, cotangent, ids_hbm, probs_hbm, gate_hbm, up_hbm, down_hbm,
    grad_gate, grad_up, grad_down,
    ids, probs, w_hidden, w_down, w_hidden_t, w_down_t, base, select, select_t, weights,
    out_a, out_b, out_r, in_a, in_b, in_r,
    carry_out, carry_in, rows, scaled_rows, work, pre_hidden,
    all_rows, all_scaled, all_back, all_act, spread,
    early_out, early_in, ids_in, probs_in, tiles_out, tiles_in,
    load_sem, send_a, send_b, send_r, recv_a, recv_b, recv_r,
    send_carry, recv_carry, send_dp, recv_dp,
    send_early, recv_early,
):
    batches, tokens_b, slots, cap, top, experts, n_dp = sizes
    width = base.shape[-1]
    units = w_down.shape[0]
    pieces = width // LANES
    part = width // n_dp
    pairs = tokens_b * top
    section = lax.axis_index("section")
    me = lax.axis_index("expert")
    z = lax.axis_index("dp")

    def expert_at(p):
        return lax.rem(me + p, experts)

    def dp_at(q):
        return lax.rem(z + q, n_dp)

    loads = [
        pltpu.make_async_copy(gate_hbm, w_hidden.at[:, pl.ds(0, units)], load_sem.at[0]),
        pltpu.make_async_copy(up_hbm, w_hidden.at[:, pl.ds(units, units)], load_sem.at[1]),
        pltpu.make_async_copy(down_hbm, w_down, load_sem.at[2]),
    ]

    @pl.when(section == 0)
    def _():
        pltpu.make_async_copy(tokens, base, load_sem.at[3]).start()

    @pl.when(section == 1)
    def _():
        pltpu.make_async_copy(cotangent, base, load_sem.at[3]).start()

    tables = [
        pltpu.make_async_copy(ids_hbm, ids, load_sem.at[4]),
        pltpu.make_async_copy(probs_hbm, probs, load_sem.at[5]),
    ]
    for load in tables + loads:
        load.start()

    barrier = pltpu.get_barrier_semaphore()

    def greet(p, _):
        pl.semaphore_signal(barrier, inc=1, device_id={"expert": expert_at(p)}, device_id_type=MESH)
        return 0

    lax.fori_loop(1, experts, greet, 0)
    for q in range(1, n_dp):
        pl.semaphore_signal(barrier, inc=1, device_id={"dp": dp_at(q)}, device_id_type=MESH)
    pl.semaphore_signal(barrier, inc=1, device_id={"section": 1 - section}, device_id_type=MESH)

    def upright(row):
        size = row.shape[-1]
        along = lax.broadcasted_iota(jnp.int32, (size, size), 1)
        down = lax.broadcasted_iota(jnp.int32, (size, size), 0)
        return jnp.sum(jnp.where(along == down, row, 0.0), 1, keepdims=True)

    def places(named_ids, by_slot=False):
        named_row = named_ids.astype(F32)
        own = jnp.concatenate([upright(named_row[k:k + 1]) for k in range(top)], 0).astype(jnp.int32)
        order_l = lax.broadcasted_iota(jnp.int32, (pairs, pairs), 1)
        order_s = lax.broadcasted_iota(jnp.int32, (pairs, pairs), 0)
        before = jnp.where(order_l < order_s, 1.0, 0.0).astype(BF16)
        one_hot = jnp.where(own == lax.broadcasted_iota(jnp.int32, (pairs, experts), 1), 1.0, 0.0)
        earlier = matmul(before, one_hot.astype(BF16))
        rank = jnp.sum(earlier * one_hot, 1, keepdims=True)
        relative = own - me
        relative = jnp.where(relative < 0, relative + experts, relative)
        relative = relative.astype(F32)
        target = rank * experts + relative if by_slot else relative * cap + rank
        target_row = jnp.sum(jnp.where(order_l == order_s, target, 0.0), 0, keepdims=True)
        return target, target_row

    def selector(target_row):
        lines = lax.broadcasted_iota(jnp.int32, (slots, pairs), 0).astype(F32)
        return jnp.where(lines == target_row, 1.0, 0.0).astype(BF16)

    def weights_of(prob_row):
        return jnp.concatenate([upright(prob_row[k:k + 1]) for k in range(top)], 0)

    def selectors(b):
        weights[b] = weights_of(probs[b])
        target, target_row = places(ids[b])
        columns = lax.broadcasted_iota(jnp.int32, (pairs, slots), 1).astype(F32)
        select_t[b] = jnp.where(columns == target, 1.0, 0.0).astype(BF16)
        select[b] = selector(target_row)

    for load in tables:
        load.wait()
    pltpu.make_async_copy(tokens, base, load_sem.at[3]).wait()

    def pack(values, out, own, b):
        for j in range(pieces):
            spread[pl.ds(j, slots, stride=pieces), :] = values[:, j * LANES:(j + 1) * LANES]
        out[b] = spread[...].reshape(slots, pieces, LANES).astype(BF16)
        own[b, 0:cap] = out[b, 0:cap]

    def unpack(tiles, ref):
        spread[...] = tiles.astype(F32).reshape(slots * pieces, LANES)
        for j in range(pieces):
            ref[:, j * LANES:(j + 1) * LANES] = spread[pl.ds(j, slots, stride=pieces), :].astype(BF16)

    chunk = cap

    def exchange(out, into, send_sem, recv_sem, b, sign):
        def one(p, _):
            place = pl.ds(p * chunk, chunk)
            to = lax.rem(me + sign * p + experts, experts)
            pltpu.make_async_remote_copy(
                src_ref=out.at[b, place], dst_ref=into.at[b, place],
                send_sem=send_sem.at[b], recv_sem=recv_sem.at[b],
                device_id={"expert": to}, device_id_type=MESH,
            ).start()
            return 0

        lax.fori_loop(1, experts, one, 0)

    def exchanged(out, into, send_sem, recv_sem, b):
        others = pl.ds(chunk, slots - chunk)
        return pltpu.make_async_remote_copy(
            src_ref=out.at[b, others], dst_ref=into.at[b, others],
            send_sem=send_sem.at[b], recv_sem=recv_sem.at[b],
            device_id={"expert": expert_at(1)}, device_id_type=MESH,
        )

    def carry(b):
        return pltpu.make_async_remote_copy(
            src_ref=carry_out.at[b], dst_ref=carry_in.at[b],
            send_sem=send_carry.at[b], recv_sem=recv_carry.at[b],
            device_id={"section": 1 - section}, device_id_type=MESH,
        )

    def to_dp(src, into, which, b, q, to):
        return pltpu.make_async_remote_copy(
            src_ref=src, dst_ref=into.at[b, q],
            send_sem=send_dp.at[which], recv_sem=recv_dp.at[which, q, b],
            device_id={"dp": to}, device_id_type=MESH,
        )

    def share_part(source, into, which, b):
        for q in sorted(range(1, n_dp), key=lambda q: -min(q, n_dp - q)):
            lanes = pl.ds(pl.multiple_of(dp_at(q) * part, part), part)
            to_dp(source.at[b, :, lanes], into, which, b, q, dp_at(q)).start()

    def share(into, which, b):
        for q in (1, n_dp - 1):
            to_dp(into.at[b, 0], into, which, b, q, dp_at(q)).start()

    def arrived(into, which, b, q):
        to_dp(into.at[b, q], into, which, b, q, dp_at(1)).wait_recv()

    def forward(into, which, b, q):
        arrived(into, which, b, q)
        to_dp(into.at[b, q], into, which, b, 2, dp_at(q)).start()

    def left(into, which):
        others = into.at[:, pl.ds(1, n_dp - 1)]
        pltpu.make_async_remote_copy(
            src_ref=others, dst_ref=others,
            send_sem=send_dp.at[which], recv_sem=recv_dp.at[which, 0, 0],
            device_id={"dp": dp_at(1)}, device_id_type=MESH,
        ).wait_send()

    pieces_part = part // LANES
    cap_all = cap * batches

    def early(src, dst, which, q, to):
        return pltpu.make_async_remote_copy(
            src_ref=src, dst_ref=dst, send_sem=send_early.at[which], recv_sem=recv_early.at[which, q],
            device_id={"dp": to}, device_id_type=MESH,
        )

    def early_tiles(q, p, sem, to):
        return pltpu.make_async_remote_copy(
            src_ref=tiles_out.at[q, p], dst_ref=tiles_in.at[q, p],
            send_sem=send_early.at[3], recv_sem=recv_early.at[3, sem],
            device_id={"expert": to}, device_id_type=MESH,
        )

    def early_send(source, b):
        for q in range(1, n_dp):
            lanes = pl.ds(pl.multiple_of(dp_at(q) * part, part), part)
            early(source.at[b, :, lanes], early_in.at[q, b], 0, q, dp_at(q)).start()

    def early_tables():
        for q in range(1, n_dp):
            early(ids, ids_in.at[q], 1, q, dp_at(q)).start()
            early(probs, probs_in.at[q], 2, q, dp_at(q)).start()

    def early_dispatch(q):
        for which, into in enumerate((early_in, ids_in, probs_in)):
            early(into.at[q], into.at[q], which, q, dp_at(1)).wait_recv()
        for b in range(batches):
            picked = selector(places(ids_in[q, b], True)[1])
            weight = weights_of(probs_in[q, b])
            values = early_in[q, b].astype(F32)
            scaled = jnp.concatenate(
                [
                    (jnp.where(section == 0, 1.0, weight[k * tokens_b:(k + 1) * tokens_b]) * values).astype(BF16)
                    for k in range(top)
                ],
                0,
            )
            out = matmul(picked, scaled)
            for slot in range(cap):
                for j in range(pieces_part):
                    spread[pl.ds(j * cap_all + b * cap + slot, experts, stride=cap_all * pieces_part), :] = out[
                        slot * experts:(slot + 1) * experts, j * LANES:(j + 1) * LANES
                    ]
        tiles_out[q] = spread[...].reshape(experts, cap_all * pieces_part, LANES).astype(BF16)
        tiles_in[q, 0] = tiles_out[q, 0]

        def one(p, _):
            early_tiles(q, p, q, expert_at(p)).start()
            return 0

        lax.fori_loop(1, experts, one, 0)

    def early_take(q):
        early_tiles(q, pl.ds(1, experts - 1), q, expert_at(1)).wait_recv()
        spread[...] = tiles_in[q].astype(F32).reshape(slots * pieces, LANES)
        down = lax.broadcasted_iota(jnp.int32, (slots, slots), 0)
        along = lax.broadcasted_iota(jnp.int32, (slots, slots), 1)
        order = jnp.where(lax.rem(down, cap) * experts + down // cap == along, 1.0, 0.0).astype(BF16)
        for b in range(batches):
            for slot in range(cap):
                for j in range(pieces_part):
                    work[slot * experts:(slot + 1) * experts, j * LANES:(j + 1) * LANES] = spread[
                        pl.ds(j * cap_all + b * cap + slot, experts, stride=cap_all * pieces_part), :
                    ].astype(BF16)
            block = matmul(order, work[:, 0:part]).astype(BF16)

            @pl.when(section == 0)
            def _():
                all_rows[b, q] = block

            @pl.when(section == 1)
            def _():
                all_scaled[b, q] = block

    mine = pl.ds(pl.multiple_of(z * part, part), part)

    def pack_rows(b, current):
        normed = (current * inverse_rms(current)).astype(BF16)
        chosen = select[b, :, 0:tokens_b] + select[b, :, tokens_b:pairs]
        pack(matmul(chosen, normed), out_a, in_a, b)
        early_out[b] = normed

    def dispatch_rows(b, current):
        pack_rows(b, current)
        send_rows(b)

    def send_rows(b):
        exchange(out_a, in_a, send_a, recv_a, b, 1)

    def pack_scaled(b, upstream):
        scaled = jnp.concatenate(
            [(weights[b, k * tokens_b:(k + 1) * tokens_b] * upstream).astype(BF16) for k in range(top)], 0
        )
        pack(matmul(select[b], scaled), out_b, in_b, b)

    def dispatch_scaled(b, upstream):
        pack_scaled(b, upstream)
        send_scaled(b)

    def send_scaled(b):
        exchange(out_b, in_b, send_b, recv_b, b, 1)

    def take_rows(b):
        exchanged(out_a, in_a, send_a, recv_a, b).wait_recv()
        unpack(in_a[b], rows.at[b])
        all_rows[b, 0] = rows[b, :, mine]

        @pl.when(section == 1)
        def _():
            share_part(rows, all_rows, 0, b)

    def take_scaled(b):
        exchanged(out_b, in_b, send_b, recv_b, b).wait_recv()
        unpack(in_b[b], scaled_rows.at[b])
        all_scaled[b, 0] = scaled_rows[b, :, mine]

        @pl.when(section == 0)
        def _():
            share_part(scaled_rows, all_scaled, 1, b)

    def hidden(b):
        pre = matmul(rows[b], w_hidden[...])
        pre_hidden[b] = pre
        g, u = pre[:, 0:units], pre[:, units:2 * units]
        all_act[b, 0] = (g * jax.nn.sigmoid(g) * u).astype(BF16)
        share(all_act, 2, b)

    def produce(b):
        pack(matmul(all_act[b, 0], w_down[...]), out_r, in_r, b)
        exchange(out_r, in_r, send_r, recv_r, b, -1)

    def hidden_back(b):
        back = matmul(scaled_rows[b], w_down_t[...])
        g, u = pre_hidden[b, :, 0:units], pre_hidden[b, :, units:2 * units]
        sg = jax.nn.sigmoid(g)
        all_back[b, 0, :, 0:units] = (back * u * sg * (1.0 + g * (1.0 - sg))).astype(BF16)
        all_back[b, 0, :, units:2 * units] = (back * (g * sg)).astype(BF16)
        share(all_back, 3, b)

    def produce_back(b):
        pack(matmul(all_back[b, 0], w_hidden_t[...]), out_r, in_r, b)
        exchange(out_r, in_r, send_r, recv_r, b, -1)

    def turn_down(b):
        place = pl.ds(pl.multiple_of(b * (width // batches), width // batches), width // batches)
        w_down_t[place, :] = w_down[:, place].T

    def turn_hidden(b):
        place = pl.ds(pl.multiple_of(b * (width // batches), width // batches), width // batches)
        w_hidden_t[:, place] = w_hidden[place, :].T

    def take_returned(b):
        exchanged(out_r, in_r, send_r, recv_r, b).wait_recv()
        unpack(in_r[b], work)
        return matmul(select_t[b], work[...])

    def combine(b):
        chosen = take_returned(b)
        total = weights[b, 0:tokens_b] * chosen[0:tokens_b]
        for k in range(1, top):
            part_k = slice(k * tokens_b, (k + 1) * tokens_b)
            total = total + weights[b, part_k] * chosen[part_k]
        carry_out[b] = (base[b].astype(F32) + total).astype(BF16)
        carry(b).start()

    def combine_back(b):
        chosen = take_returned(b)
        d_normed = chosen[0:tokens_b]
        for k in range(1, top):
            d_normed = d_normed + chosen[k * tokens_b:(k + 1) * tokens_b]
        current = carry_in[b].astype(F32)
        scale = inverse_rms(current)
        back = scale * d_normed - current * (scale * scale * scale) * jnp.mean(
            d_normed * current, -1, keepdims=True
        )
        carry_out[b] = (base[b].astype(F32) + back).astype(BF16)
        carry(b).start()

    def forward_act(b):
        @pl.when(lax.rem(b, 2) == 0)
        def _():
            forward(all_act, 2, b, 1)

        @pl.when(lax.rem(b, 2) == 1)
        def _():
            forward(all_act, 2, b, n_dp - 1)

    def forward_back(b):
        for q, lanes in ((1, pl.ds(0, units)), (n_dp - 1, pl.ds(units, units))):
            arrived(all_back, 3, b, q)
            pltpu.make_async_remote_copy(
                src_ref=all_back.at[b, q, :, lanes], dst_ref=all_back.at[b, 2, :, lanes],
                send_sem=send_dp.at[3], recv_sem=recv_dp.at[3, 2, b],
                device_id={"dp": dp_at(q)}, device_id_type=MESH,
            ).start()

    def all_arrived(b):
        @pl.when(section == 0)
        def _():
            for q in range(1, n_dp):
                arrived(all_scaled, 1, b, q)

        @pl.when(section == 1)
        def _():
            for q in range(1, n_dp):
                arrived(all_rows, 0, b, q)

        @pl.when(lax.rem(b, 2) == 0)
        def _():
            arrived(all_act, 2, b, n_dp - 1)

        @pl.when(lax.rem(b, 2) == 1)
        def _():
            arrived(all_act, 2, b, 1)

        arrived(all_act, 2, b, 2)
        arrived(all_back, 3, b, 2)

    def wait_loads():
        for load in loads:
            load.wait()

    def loop(count, body, first=0):
        def step(i, _):
            body(i)
            return 0

        lax.fori_loop(first, count, step, 0)

    selectors(0)

    @pl.when(section == 0)
    def _():
        pack_rows(0, base[0].astype(F32))

    @pl.when(section == 1)
    def _():
        pack_scaled(0, base[0].astype(F32))

    pl.semaphore_wait(barrier, experts - 1 + n_dp - 1 + 1)

    @pl.when(section == 0)
    def _():
        def start(b):
            selectors(b)
            dispatch_rows(b, base[b].astype(F32))
            early_send(early_out, b)

        send_rows(0)
        early_send(early_out, 0)
        early_tables()
        loop(batches, start, 1)
        wait_loads()

        def forward_step(i):
            @pl.when(i < batches)
            def _():
                take_rows(i)
                hidden(i)
                produce(i)

            @pl.when(i >= 1)
            def _():
                combine(i - 1)

        loop(batches + 1, forward_step)
        loop(batches, turn_down)
        loop(n_dp, early_dispatch, 1)

        def backward(i):
            @pl.when(i < batches)
            def _():
                carry(i).wait_recv()
                dispatch_scaled(i, carry_in[i].astype(F32))
                forward_act(i)

            @pl.when(i >= 1)
            def _():
                take_scaled(i - 1)
                hidden_back(i - 1)

            @pl.when(i >= 2)
            def _():
                forward_back(i - 2)

            @pl.when((i >= 1) & (i < n_dp))
            def _():
                early_take(i)

        loop(batches + 1, backward)

    @pl.when(section == 1)
    def _():
        def start(b):
            selectors(b)
            dispatch_scaled(b, base[b].astype(F32))
            early_send(base, b)

        send_scaled(0)
        loop(batches, lambda b: early_send(base, b))
        early_tables()

        def start(b):
            selectors(b)
            pack_scaled(b, base[b].astype(F32))

        loop(batches, start, 1)
        loop(2, send_scaled, 1)
        wait_loads()
        loop(batches, turn_down)
        loop(batches, turn_hidden)

        def both(i):
            @pl.when(i < batches)
            def _():
                carry(i).wait_recv()
                dispatch_rows(i, carry_in[i].astype(F32))

            @pl.when(i + 2 < batches)
            def _():
                send_scaled(i + 2)

            @pl.when((i >= 1) & (i < batches + 1))
            def _():
                take_rows(i - 1)
                hidden(i - 1)
                take_scaled(i - 1)
                hidden_back(i - 1)
                produce_back(i - 1)

            @pl.when(i >= 2)
            def _():
                combine_back(i - 2)
                forward_act(i - 2)
                forward_back(i - 2)

        loop(batches + 2, both)
        loop(n_dp, early_dispatch, 1)

    def add_up(b):
        all_arrived(b)

        def flat(ref):
            return ref[b].reshape(n_dp * slots, ref.shape[-1])

        both = matmul(flat(all_rows), flat(all_back), rows_by_rows)
        gate_part, up_part = both[:, 0:units], both[:, units:2 * units]
        down_part = matmul(flat(all_act), flat(all_scaled), rows_by_rows)

        @pl.when(b == 0)
        def _():
            grad_gate[...] = gate_part
            grad_up[...] = up_part
            grad_down[...] = down_part

        @pl.when(b > 0)
        def _():
            grad_gate[...] += gate_part
            grad_up[...] += up_part
            grad_down[...] += down_part

    @pl.when(section == 1)
    def _():
        loop(n_dp, early_take, 1)

    def finish(b):
        add_up(b)

        @pl.when((section == 0) & (b == 1))
        def _():
            forward_back(batches - 1)

    loop(batches, finish)

    def sent(b):
        exchanged(out_a, in_a, send_a, recv_a, b).wait_send()
        exchanged(out_b, in_b, send_b, recv_b, b).wait_send()
        exchanged(out_r, in_r, send_r, recv_r, b).wait_send()
        carry(b).wait_send()

    loop(batches, sent)
    @pl.when(section == 0)
    def _():
        left(all_scaled, 1)

    @pl.when(section == 1)
    def _():
        left(all_rows, 0)

    for which, into in enumerate((early_in, ids_in, probs_in)):
        early(into.at[pl.ds(1, n_dp - 1)], into.at[pl.ds(1, n_dp - 1)], which, 0, dp_at(1)).wait_send()
    early_tiles(pl.ds(1, n_dp - 1), pl.ds(1, experts - 1), 0, expert_at(1)).wait_send()
    left(all_act, 2)
    left(all_back, 3)


def hand_over(*refs):
    copies = [pltpu.make_async_copy(refs[i], refs[3 + i], refs[6].at[i]) for i in range(3)]
    for copy in copies:
        copy.start()
    for copy in copies:
        copy.wait()


def shards(tokens, routes, gate_probs, w_gate, w_up, w_down, cotangent):
    micro_count, row_count, width = tokens.shape
    top = routes.shape[-1]
    experts = lax.axis_size("expert")
    n_dp = lax.axis_size("dp")
    cap = min(row_count, row_count * top // experts + 1)
    hidden = w_gate.shape[-1]
    batches, tokens_b = micro_count, row_count
    slots = experts * cap
    pieces = width // LANES
    part = width // n_dp

    def in_hbm(array):
        return pltpu.with_memory_space_constraint(array, pltpu.HBM)

    any_ = pl.BlockSpec(memory_space=pl.ANY)
    vmem = pl.BlockSpec(memory_space=pltpu.VMEM)
    dma = pltpu.SemaphoreType.DMA
    outs = pl.pallas_call(
        functools.partial(kernel, (batches, tokens_b, slots, cap, top, experts, n_dp)),
        out_shape=[
            jax.ShapeDtypeStruct((part, hidden), F32),
            jax.ShapeDtypeStruct((part, hidden), F32),
            jax.ShapeDtypeStruct((hidden, part), F32),
        ],
        in_specs=[any_] * 7,
        out_specs=[vmem] * 3,
        scratch_shapes=[
            pltpu.VMEM((batches, top, tokens_b), jnp.int32),
            pltpu.VMEM((batches, top, tokens_b), F32),
            pltpu.VMEM((width, 2 * hidden), BF16),
            pltpu.VMEM((hidden, width), BF16),
            pltpu.VMEM((2 * hidden, width), BF16),
            pltpu.VMEM((width, hidden), BF16),
            pltpu.VMEM((batches, tokens_b, width), BF16),
            pltpu.VMEM((batches, slots, tokens_b * top), BF16),
            pltpu.VMEM((batches, tokens_b * top, slots), BF16),
            pltpu.VMEM((batches, tokens_b * top, 1), F32),
            *[pltpu.VMEM((batches, slots, pieces, LANES), BF16)] * 6,
            *[pltpu.VMEM((batches, tokens_b, width), BF16)] * 2,
            *[pltpu.VMEM((batches, slots, width), BF16)] * 2,
            pltpu.VMEM((slots, width), BF16),
            pltpu.VMEM((batches, slots, 2 * hidden), F32),
            *[pltpu.VMEM((batches, n_dp, slots, part), BF16)] * 2,
            pltpu.VMEM((batches, n_dp, slots, 2 * hidden), BF16),
            pltpu.VMEM((batches, n_dp, slots, hidden), BF16),
            pltpu.VMEM((slots * pieces, LANES), F32),
            pltpu.VMEM((batches, tokens_b, width), BF16),
            pltpu.VMEM((n_dp, batches, tokens_b, part), BF16),
            pltpu.VMEM((n_dp, batches, top, tokens_b), jnp.int32),
            pltpu.VMEM((n_dp, batches, top, tokens_b), F32),
            *[pltpu.VMEM((n_dp, experts, cap * batches * part // LANES, LANES), BF16)] * 2,
            dma((6,)),
            *[dma((batches,))] * 6,
            *[dma((batches,))] * 2,
            dma((4,)),
            dma((4, n_dp, batches)),
            dma((4,)),
            dma((4, n_dp)),
        ],
        compiler_params=pltpu.CompilerParams(
            collective_id=0, has_side_effects=True, vmem_limit_bytes=50 * 1024 * 1024
        ),
    )(
        in_hbm(tokens), in_hbm(cotangent),
        in_hbm(routes[0].transpose(0, 2, 1)), in_hbm(gate_probs[0].transpose(0, 2, 1)),
        in_hbm(w_gate[0, 0]), in_hbm(w_up[0, 0]), in_hbm(w_down[0, 0]),
    )
    outs = pl.pallas_call(
        hand_over,
        out_shape=[pltpu.HBM(out.shape, out.dtype) for out in outs],
        in_specs=[any_] * 3,
        out_specs=[any_] * 3,
        scratch_shapes=[dma((3,))],
        compiler_params=pltpu.CompilerParams(vmem_limit_bytes=4 * 1024 * 1024),
    )(*outs)
    return tuple(out[None, None] for out in outs)


def solution(mesh):
    in_specs = (
        P(None, ("expert", "dp"), None),
        P("section", None, ("expert", "dp"), None),
        P("section", None, ("expert", "dp"), None),
        P("section", "expert", None, None),
        P("section", "expert", None, None),
        P("section", "expert", None, None),
        P(None, ("expert", "dp"), None),
    )
    out_specs = (
        P("section", "expert", "dp", None),
        P("section", "expert", "dp", None),
        P("section", "expert", None, "dp"),
    )
    return jax.shard_map(shards, mesh=mesh, in_specs=in_specs, out_specs=out_specs, check_vma=False)
```
